768 devices in a mesh: user: 64 (over x, y, core), item: 12 (over z).
Axes of the slice: x: 4, y: 8, z: 12, core: 2. Of those that a mesh axis runs over, the one named last changes fastest.
Arguments:
- ratings: bfloat16 [24576, 3072], P('user', 'item'), may hold values from -64 to 64
- counts: int32 [384], P('user'), may hold values from 0 to 64, as said below
Outputs:
- similarity: bfloat16 [3072, 3072], P('user', 'item')
The draws below stay inside these ranges and needn't reach their ends.
Inputs may be any that keep to these rules, and one draw needn't show every extreme that they name: `counts`: live rows of each aligned block of 64 user rows; rows at or past the count are padding; each index of user holds a block with 64 live rows.
All inputs are finite; a program needn't handle non-finite values.
Results may differ from the reference program's by a relative error of at most 0.0034.
Values may be sent and summed in bfloat16 or wider, within the bound.
No kernel may reach another device: no remote copies, remote signals or barrier semaphores. Data moves between devices by JAX's collectives and lax.ppermute only.
A program may use at most 32 MiB of HBM per device.

```python
import jax
import jax.numpy as jnp
from jax import lax

ITEMS_DEV = 256
U_DEV = 384
BLK = 64
N_USER = 64
N_ITEM = 12


def draw_ratings(key, part):
    key = jax.random.fold_in(key, 11)
    subkeys = jax.random.split(key, 8)
    user_total = U_DEV * N_USER
    item_total = ITEMS_DEV * N_ITEM
    user_pos = jnp.arange(user_total)
    item_pos = jnp.arange(item_total)
    noise = jnp.clip(jax.random.normal(subkeys[0], (user_total, item_total)), -4.0, 4.0)
    common = 0.15
    far_shift = ITEMS_DEV // 2 + 3
    mixed = noise + 0.6 * jnp.roll(noise, 1, axis=1) + 0.45 * jnp.roll(noise, far_shift, axis=1)
    first_user = jax.random.normal(subkeys[1], (user_total,))
    first_item = jax.random.normal(subkeys[2], (item_total,))
    second_user = jax.random.normal(subkeys[3], (user_total,))
    second_item = jax.random.normal(subkeys[4], (item_total,))
    core = mixed + common * first_user[:, None] * first_item[None, :] + 0.1 * second_user[:, None] * second_item[None, :]
    owner = jax.random.permutation(subkeys[5], N_USER)[user_pos // U_DEV]
    slice_of = item_pos // (item_total // N_USER)
    core = core * jnp.where(slice_of[None, :] == owner[:, None], 4.0, 1.0)
    row_scale = 3.0 ** (user_pos / user_total) * jnp.exp(jax.random.uniform(subkeys[6], (user_total,), minval=-1.15, maxval=1.15))
    col_scale = 3.0 ** (item_pos / item_total) * jnp.exp(jax.random.uniform(subkeys[7], (item_total,), minval=-1.15, maxval=1.15))
    values = core * 0.25 * row_scale[:, None] * col_scale[None, :]
    return jnp.clip(values, -64.0, 64.0).astype(jnp.bfloat16)


def draw_counts(key, part):
    key = jax.random.fold_in(key, 23)
    subkeys = jax.random.split(key, 2)
    block_count = U_DEV // BLK
    raw_live = jax.random.randint(subkeys[0], (N_USER, block_count), -(BLK // 2), BLK + 1)
    live_count = jnp.maximum(raw_live, 0)
    full_block = jax.random.randint(subkeys[1], (N_USER,), 0, block_count)
    live_count = jnp.where(jnp.arange(block_count)[None, :] == full_block[:, None], BLK, live_count)
    return live_count.reshape(-1).astype(jnp.int32)


def setup_inputs(seed: int = 0) -> dict:
    seeds = jax.random.split(jax.random.key(seed), 3)
    return {
        "ratings": draw_ratings(jax.random.fold_in(seeds[2], 71), 0),
        "counts": draw_counts(jax.random.fold_in(seeds[2], 71), 0),
    }


def reference(ratings, counts):
    row_count = ratings.shape[0]
    live_rows = (jnp.arange(row_count) % BLK < jnp.repeat(counts, BLK)).astype(jnp.float32)
    values = ratings.astype(jnp.float32)
    mean_square = lax.optimization_barrier(jnp.sum(values * values, axis=1)) / ratings.shape[1]
    user_scale = live_rows / jnp.sqrt(mean_square + 1e-05)
    weighted = (user_scale[:, None] * values).astype(jnp.bfloat16)
    gram = lax.dot_general(ratings, weighted, (((0,), (0,)), ((), ())), preferred_element_type=jnp.float32)
    degree = lax.optimization_barrier(jnp.sum(values * weighted.astype(jnp.float32), axis=0))
    inverse_root = 1.0 / jnp.sqrt(degree)
    return (gram * inverse_root[:, None] * inverse_root[None, :]).astype(jnp.bfloat16)
```

```python
import functools

import jax
import jax.numpy as jnp
from jax import lax
from jax.experimental import pallas as pl
from jax.experimental.pallas import tpu as pltpu
from jax.sharding import Mesh, PartitionSpec as P

X, Y, CORES, PANELS = 4, 8, 2, 12
SLOTS = X * Y
BLOCK = 64
ITEMS = 3072
SHARE = 48
SLOT_ROWS = SHARE + 8


def split_rows(total):
    high = total.astype(jnp.bfloat16).astype(jnp.float32)
    first = lax.broadcasted_iota(jnp.int32, total.shape, 0) < 4
    return jnp.where(first, high, total - high)


def partial_kernel(place_ref, counts_ref, *refs):
    panels, (keep_ref, send_ref, gram_ref, degree_ref) = refs[:PANELS], refs[PANELS:]
    me, core = place_ref[0], place_ref[1]
    rows, width = panels[0].shape
    squares = jnp.zeros((rows, width), jnp.float32)
    for panel in panels:
        values = panel[...].astype(jnp.float32)
        squares = squares + values * values
    square_sum = jnp.sum(squares, axis=1, keepdims=True)
    position = lax.broadcasted_iota(jnp.int32, (BLOCK, 1), 0)
    live = jnp.concatenate(
        [(position < counts_ref[i]).astype(jnp.float32) for i in range(rows // BLOCK)], axis=0
    )
    scale = live / jnp.sqrt(square_sum / ITEMS + 1e-05)
    weighted = (scale * panels[0][...].astype(jnp.float32)).astype(jnp.bfloat16)
    for k, panel in enumerate(panels):
        owner = lax.rem(me + k, PANELS)
        product = lax.dot_general(
            panel[...], weighted, (((0,), (0,)), ((), ())), preferred_element_type=jnp.float32
        )
        gram_ref[pl.ds(pl.multiple_of(owner * width, width), width), :] = product
        values = panel[...].astype(jnp.float32)
        own_weighted = (scale * values).astype(jnp.bfloat16).astype(jnp.float32)
        degree_ref[pl.ds(owner, 1), :] = jnp.sum(values * own_weighted, axis=0, keepdims=True)
    column_degree = degree_ref[pl.ds(me, 1), :]
    blank = jnp.zeros((1, width), jnp.float32)
    for slot in range(SLOTS):
        for mine in (True, False):
            start = (2 * slot + (core if mine else 1 - core)) * SHARE
            low = degree_ref[pl.ds(lax.shift_right_logical(start, 8), 1), :]
            high = degree_ref[pl.ds(lax.shift_right_logical(start + SHARE - 1, 8), 1), :]
            block = gram_ref[pl.ds(pl.multiple_of(start, 16), SHARE), :]
            four = [column_degree, low, high, blank]
            if mine:
                extra = jnp.concatenate(four + [blank] * 4, axis=0)
                keep_ref[slot] = jnp.concatenate([block, extra], axis=0)
            else:
                extra = split_rows(jnp.concatenate(four + four, axis=0))
                send_ref[slot] = jnp.concatenate([block, extra], axis=0).astype(jnp.bfloat16)


def add_kernel(keep_ref, got_ref, out_ref):
    for slot in range(SLOTS):
        total = keep_ref[slot] + got_ref[slot].astype(jnp.float32)
        extra = total[SHARE:]
        extra = split_rows(extra + pltpu.roll(extra, 4, 0))
        out_ref[slot] = jnp.concatenate([total[:SHARE], extra], axis=0).astype(jnp.bfloat16)


def finish_kernel(place_ref, got_ref, out_ref):
    start = place_ref[2] * SHARE
    offset = start - lax.shift_left(lax.shift_right_logical(start, 8), 8)
    total = got_ref[0].astype(jnp.float32)
    for slot in range(1, SLOTS):
        total = total + got_ref[slot].astype(jnp.float32)
    extra = total[SHARE:]
    extra = extra + pltpu.roll(extra, 4, 0)
    width = total.shape[1]
    lane = lax.broadcasted_iota(jnp.int32, (SHARE, width), 1)
    row = lax.broadcasted_iota(jnp.int32, (SHARE, width), 0) + offset
    row_degree = jnp.sum(
        jnp.where(lane == row, extra[1:2], 0.0) + jnp.where(lane + width == row, extra[2:3], 0.0),
        axis=1,
        keepdims=True,
    )
    row_inverse = 1.0 / jnp.sqrt(row_degree)
    column_inverse = 1.0 / jnp.sqrt(extra[0:1])
    out_ref[...] = (total[:SHARE] * row_inverse * column_inverse).astype(jnp.bfloat16)


VMEM = pl.BlockSpec(memory_space=pltpu.VMEM)
SMEM = pl.BlockSpec(memory_space=pltpu.SMEM)
PARAMS = pltpu.CompilerParams(vmem_limit_bytes=48 * 1024 * 1024)


def per_device(ratings, counts):
    width = ratings.shape[1]
    x, y, core, me = (lax.axis_index(name) for name in ("x", "y", "core", "z"))
    place = jnp.stack([me, core, (x * Y + y) * CORES + core]).astype(jnp.int32)

    def step(array, by):
        return lax.ppermute(array, "z", [(i, (i + by) % PANELS) for i in range(PANELS)])

    panels = [ratings] + [None] * (PANELS - 1)
    up = down = ratings
    for hop in range(1, 7):
        up = step(up, 1)
        panels[PANELS - hop] = up
        if hop < 6:
            down = step(down, -1)
            panels[hop] = down
    slots = (SLOTS, SLOT_ROWS, width)
    keep, send = pl.pallas_call(
        partial_kernel,
        out_shape=(
            jax.ShapeDtypeStruct(slots, jnp.float32),
            jax.ShapeDtypeStruct(slots, jnp.bfloat16),
        ),
        in_specs=[SMEM, SMEM] + [VMEM] * PANELS,
        out_specs=(VMEM, VMEM),
        scratch_shapes=[
            pltpu.VMEM((ITEMS, width), jnp.float32),
            pltpu.VMEM((16, width), jnp.float32),
        ],
        compiler_params=PARAMS,
        name="partial",
    )(place, counts, *panels)
    got = lax.ppermute(send, "core", [(0, 1), (1, 0)])
    total = pl.pallas_call(
        add_kernel,
        out_shape=jax.ShapeDtypeStruct(slots, jnp.bfloat16),
        in_specs=[VMEM, VMEM],
        out_specs=VMEM,
        compiler_params=PARAMS,
        name="add",
    )(keep, got)
    parts = lax.all_to_all(total, ("x", "y"), 0, 0, tiled=True)
    return pl.pallas_call(
        finish_kernel,
        out_shape=jax.ShapeDtypeStruct((SHARE, width), jnp.bfloat16),
        in_specs=[SMEM, VMEM],
        out_specs=VMEM,
        compiler_params=PARAMS,
        name="finish",
    )(place, parts)


def solution(mesh):
    fine = Mesh(mesh.devices.reshape(X, Y, CORES, PANELS), ("x", "y", "core", "z"))
    users = ("x", "y", "core")
    return jax.shard_map(
        per_device,
        mesh=fine,
        in_specs=(P(users, "z"), P(users)),
        out_specs=P(users, "z"),
        check_vma=False,
    )
```

```python
import functools

import jax
import jax.numpy as jnp
from jax import lax
from jax.experimental import pallas as pl
from jax.experimental.pallas import tpu as pltpu
from jax.sharding import Mesh, PartitionSpec as P

X, Y, CORES, PANELS = 4, 8, 2, 12
SLOTS = X * Y
BLOCK = 64
ITEMS = 3072
SHARE = 48
SLOT_ROWS = SHARE + 8
COUNTS = 4


def split_rows(total):
    high = total.astype(jnp.bfloat16).astype(jnp.float32)
    first = lax.broadcasted_iota(jnp.int32, total.shape, 0) < 4
    return jnp.where(first, high, total - high)


def partial_kernel(place_ref, ratings_ref, *refs):
    others, scratch = refs[: PANELS - 1], refs[PANELS - 1 :]
    keep_ref, send_ref, gram_ref, degree_ref, own_ref, fetched = scratch
    fetch = pltpu.make_async_copy(ratings_ref, own_ref, fetched)
    fetch.start()
    panels = (own_ref,) + others
    me, core = place_ref[0], place_ref[1]
    rows, width = own_ref.shape
    squares = jnp.zeros((rows, width), jnp.float32)
    for panel in others + (own_ref,):
        if panel is own_ref:
            fetch.wait()
        values = panel[...].astype(jnp.float32)
        squares = squares + values * values
    square_sum = jnp.sum(squares, axis=1, keepdims=True)
    position = lax.broadcasted_iota(jnp.int32, (BLOCK, 1), 0)
    live = jnp.concatenate(
        [(position < place_ref[COUNTS + i]).astype(jnp.float32) for i in range(rows // BLOCK)], axis=0
    )
    scale = live / jnp.sqrt(square_sum / ITEMS + 1e-05)
    weighted = (scale * panels[0][...].astype(jnp.float32)).astype(jnp.bfloat16)
    for k, panel in enumerate(panels):
        owner = lax.rem(me + k, PANELS)
        product = lax.dot_general(
            panel[...], weighted, (((0,), (0,)), ((), ())), preferred_element_type=jnp.float32
        )
        gram_ref[pl.ds(pl.multiple_of(owner * width, width), width), :] = product
        values = panel[...].astype(jnp.float32)
        own_weighted = (scale * values).astype(jnp.bfloat16).astype(jnp.float32)
        degree_ref[pl.ds(owner, 1), :] = jnp.sum(values * own_weighted, axis=0, keepdims=True)
    column_degree = degree_ref[pl.ds(me, 1), :]
    blank = jnp.zeros((1, width), jnp.float32)
    for slot in range(SLOTS):
        for mine in (True, False):
            start = (2 * slot + (core if mine else 1 - core)) * SHARE
            low = degree_ref[pl.ds(lax.shift_right_logical(start, 8), 1), :]
            high = degree_ref[pl.ds(lax.shift_right_logical(start + SHARE - 1, 8), 1), :]
            block = gram_ref[pl.ds(pl.multiple_of(start, 16), SHARE), :]
            four = [column_degree, low, high, blank]
            if mine:
                extra = jnp.concatenate(four + [blank] * 4, axis=0)
                keep_ref[slot] = jnp.concatenate([block, extra], axis=0)
            else:
                extra = split_rows(jnp.concatenate(four + four, axis=0))
                send_ref[slot] = jnp.concatenate([block, extra], axis=0).astype(jnp.bfloat16)


def add_kernel(place_ref, keep_ref, got_ref, own_ref, *send_refs):
    x = place_ref[3]
    for by, ref in enumerate((own_ref,) + send_refs):
        first = lax.rem(x + by, X) * Y
        for j in range(Y):
            total = keep_ref[first + j] + got_ref[first + j].astype(jnp.float32)
            extra = total[SHARE:]
            extra = extra + pltpu.roll(extra, 4, 0)
            if by:
                extra = split_rows(extra)
            else:
                extra = 0.5 * extra
            ref[j] = jnp.concatenate([total[:SHARE], extra], axis=0).astype(ref.dtype)


def fold_kernel(own_ref, *refs):
    out_ref = refs[-1]
    for j in range(Y):
        total = own_ref[j]
        for ref in refs[:-1]:
            total = total + ref[j].astype(jnp.float32)
        extra = total[SHARE:]
        extra = split_rows(extra + pltpu.roll(extra, 4, 0))
        out_ref[j] = jnp.concatenate([total[:SHARE], extra], axis=0).astype(jnp.bfloat16)


def finish_kernel(place_ref, got_ref, out_ref):
    start = place_ref[2] * SHARE
    offset = start - lax.shift_left(lax.shift_right_logical(start, 8), 8)
    total = got_ref[0].astype(jnp.float32)
    for slot in range(1, Y):
        total = total + got_ref[slot].astype(jnp.float32)
    extra = total[SHARE:]
    extra = extra + pltpu.roll(extra, 4, 0)
    width = total.shape[1]
    lane = lax.broadcasted_iota(jnp.int32, (SHARE, width), 1)
    row = lax.broadcasted_iota(jnp.int32, (SHARE, width), 0) + offset
    row_degree = jnp.sum(
        jnp.where(lane == row, extra[1:2], 0.0) + jnp.where(lane + width == row, extra[2:3], 0.0),
        axis=1,
        keepdims=True,
    )
    row_inverse = 1.0 / jnp.sqrt(row_degree)
    column_inverse = 1.0 / jnp.sqrt(extra[0:1])
    out_ref[...] = (total[:SHARE] * row_inverse * column_inverse).astype(jnp.bfloat16)


VMEM = pl.BlockSpec(memory_space=pltpu.VMEM)
SMEM = pl.BlockSpec(memory_space=pltpu.SMEM)
PARAMS = pltpu.CompilerParams(vmem_limit_bytes=48 * 1024 * 1024)


def per_device(ratings, counts):
    width = ratings.shape[1]
    x, y, core, me = (lax.axis_index(name) for name in ("x", "y", "core", "z"))
    place = jnp.stack([me, core, (x * Y + y) * CORES + core, x]).astype(jnp.int32)
    place = jnp.concatenate([place, counts])

    def step(array, by, axis="z", size=PANELS):
        return lax.ppermute(array, axis, [(i, (i + by) % size) for i in range(size)])

    panels = [ratings] + [None] * (PANELS - 1)
    up = down = ratings
    for hop in range(1, 7):
        up = step(up, 1)
        panels[PANELS - hop] = up
        if hop < 6:
            down = step(down, -1)
            panels[hop] = down
    slots = (SLOTS, SLOT_ROWS, width)
    keep, send = pl.pallas_call(
        partial_kernel,
        out_shape=(
            jax.ShapeDtypeStruct(slots, jnp.float32),
            jax.ShapeDtypeStruct(slots, jnp.bfloat16),
        ),
        in_specs=[SMEM, pl.BlockSpec(memory_space=pltpu.HBM)] + [VMEM] * (PANELS - 1),
        out_specs=(VMEM, VMEM),
        scratch_shapes=[
            pltpu.VMEM((ITEMS, width), jnp.float32),
            pltpu.VMEM((16, width), jnp.float32),
            pltpu.VMEM(ratings.shape, ratings.dtype),
            pltpu.SemaphoreType.DMA,
        ],
        compiler_params=PARAMS,
        name="partial",
    )(place, *panels)
    got = lax.ppermute(send, "core", [(0, 1), (1, 0)])
    quarter = (Y, SLOT_ROWS, width)
    own, *parts = pl.pallas_call(
        add_kernel,
        out_shape=(jax.ShapeDtypeStruct(quarter, jnp.float32),)
        + (jax.ShapeDtypeStruct(quarter, jnp.bfloat16),) * (X - 1),
        in_specs=[SMEM, VMEM, VMEM],
        out_specs=(VMEM,) * X,
        compiler_params=PARAMS,
        name="add",
    )(place, keep, got)
    parts = [step(part, by, "x", X) for by, part in enumerate(parts, 1)]
    total = pl.pallas_call(
        fold_kernel,
        out_shape=jax.ShapeDtypeStruct(quarter, jnp.bfloat16),
        in_specs=[VMEM] * X,
        out_specs=VMEM,
        compiler_params=PARAMS,
        name="fold",
    )(own, *parts)
    parts = lax.all_to_all(total, "y", 0, 0, tiled=True)
    return pl.pallas_call(
        finish_kernel,
        out_shape=jax.ShapeDtypeStruct((SHARE, width), jnp.bfloat16),
        in_specs=[SMEM, VMEM],
        out_specs=VMEM,
        compiler_params=PARAMS,
        name="finish",
    )(place, parts)


def solution(mesh):
    fine = Mesh(mesh.devices.reshape(X, Y, CORES, PANELS), ("x", "y", "core", "z"))
    users = ("x", "y", "core")
    return jax.shard_map(
        per_device,
        mesh=fine,
        in_specs=(P(users, "z"), P(users)),
        out_specs=P(users, "z"),
        check_vma=False,
    )
```

```python
import jax
import jax.numpy as jnp
from jax import lax
from jax.experimental import pallas as pl
from jax.experimental.pallas import tpu as pltpu
from jax.sharding import Mesh, PartitionSpec as P

X, Y, CORES, PANELS = 4, 8, 2, 12
SLOTS = X * Y
BLOCK = 64
ITEMS = 3072
SHARE = 48
SLOT_ROWS = SHARE + 8
HOPS = 4
CORE, RESIDUE, SLAB, COUNTS = 0, 1, 2, 3
UNITS = {
    (0, 0): (3, (4, 3)),
    (0, 1): (1, (2, 0)),
    (0, 2): (2, (3, 2)),
    (1, 0): (0, (-4, -3)),
    (1, 1): (1, (-1, 1)),
    (1, 2): (-1, (-1, 0)),
}


def split_rows(total):
    high = total.astype(jnp.bfloat16).astype(jnp.float32)
    first = lax.broadcasted_iota(jnp.int32, total.shape, 0) < 4
    return jnp.where(first, high, total - high)


def pair_kernel(place_ref, own_ref, other_ref, out_ref):
    core, rows = place_ref[CORE], own_ref.shape[0]
    out_ref[pl.ds(pl.multiple_of(core * rows, 64), rows), :] = own_ref[...]
    out_ref[pl.ds(pl.multiple_of((1 - core) * rows, 64), rows), :] = other_ref[...]


def partial_kernel(place_ref, near_ref, far_ref, *refs):
    panels, (out_ref, gram_ref, degree_ref) = refs[: 2 * HOPS], refs[2 * HOPS :]
    core, residue = place_ref[CORE], place_ref[RESIDUE]
    rows, width = panels[0].shape
    squares = jnp.zeros((rows, width), jnp.float32)
    for k in (3, 4, 6, 7):
        values = panels[k][...].astype(jnp.float32)
        squares = squares + values * values
    square_sum = jnp.sum(squares, axis=1, keepdims=True)
    chunk = near_ref.shape[1]
    corner = lax.broadcasted_iota(jnp.int32, (chunk, chunk), 0) == lax.broadcasted_iota(
        jnp.int32, (chunk, chunk), 1
    )
    upright = [
        jnp.sum(
            jnp.where(corner, near_ref[pl.ds(i, 1), :] + far_ref[pl.ds(i, 1), :], 0.0),
            axis=1,
            keepdims=True,
        )
        for i in range(rows // chunk)
    ]
    square_sum = square_sum + jnp.concatenate(upright, axis=0)
    position = lax.broadcasted_iota(jnp.int32, (BLOCK, 1), 0)
    blocks = rows // BLOCK // CORES
    live = []
    for i in range(CORES * blocks):
        own = core == i // blocks
        count = jnp.where(
            own, place_ref[COUNTS + i % blocks], place_ref[COUNTS + blocks + i % blocks]
        )
        live.append((position < count).astype(jnp.float32))
    scale = jnp.concatenate(live, axis=0) / jnp.sqrt(square_sum / ITEMS + 1e-05)

    for (its_core, its_residue), (at, columns) in UNITS.items():

        @pl.when((core == its_core) & (residue == its_residue))
        def _():
            def panel(offset):
                hop = -offset if its_core else offset
                return panels[hop if hop >= 0 else HOPS - hop]

            def degree(ref):
                values = ref[...].astype(jnp.float32)
                weighted = (scale * values).astype(jnp.bfloat16)
                total = jnp.sum(values * weighted.astype(jnp.float32), axis=0, keepdims=True)
                return weighted, total

            row_panels = [panel(i - at) for i in range(3)]
            for i, ref in enumerate(row_panels):
                total = degree(ref)[1]
                for unit in range(2):
                    degree_ref[pl.ds(4 * unit + 1 + i, 1), :] = total
            for unit, offset in enumerate(columns):
                weighted, total = degree(panel(offset))
                degree_ref[pl.ds(4 * unit, 1), :] = total
                for i, ref in enumerate(row_panels):
                    gram_ref[pl.ds((3 * unit + i) * width, width), :] = lax.dot_general(
                        ref[...],
                        weighted,
                        (((0,), (0,)), ((), ())),
                        preferred_element_type=jnp.float32,
                    )

    blank = jnp.zeros((1, width), jnp.float32)
    for x in range(X):
        for y in range(Y):
            unit, start = x // 2, (2 * y + x % 2) * SHARE
            low, high = start // width, (start + SHARE - 1) // width
            four = [degree_ref[pl.ds(4 * unit + i, 1), :] for i in (0, 1 + low, 1 + high)]
            four.append(blank)
            extra = split_rows(jnp.concatenate(four + four, axis=0))
            block = gram_ref[pl.ds(unit * 3 * width + start, SHARE), :]
            out_ref[x * Y + y] = jnp.concatenate([block, extra], axis=0).astype(jnp.bfloat16)


def finish_kernel(place_ref, got_ref, out_ref):
    start = place_ref[SLAB] * SHARE
    offset = start - lax.shift_left(lax.shift_right_logical(start, 8), 8)
    total = got_ref[0].astype(jnp.float32)
    for slot in range(1, SLOTS):
        total = total + got_ref[slot].astype(jnp.float32)
    extra = total[SHARE:]
    extra = extra + pltpu.roll(extra, 4, 0)
    width = total.shape[1]
    lane = lax.broadcasted_iota(jnp.int32, (SHARE, width), 1)
    row = lax.broadcasted_iota(jnp.int32, (SHARE, width), 0) + offset
    row_degree = jnp.sum(
        jnp.where(lane == row, extra[1:2], 0.0) + jnp.where(lane + width == row, extra[2:3], 0.0),
        axis=1,
        keepdims=True,
    )
    row_inverse = 1.0 / jnp.sqrt(row_degree)
    column_inverse = 1.0 / jnp.sqrt(extra[0:1])
    out_ref[...] = (total[:SHARE] * row_inverse * column_inverse).astype(jnp.bfloat16)


VMEM = pl.BlockSpec(memory_space=pltpu.VMEM)
SMEM = pl.BlockSpec(memory_space=pltpu.SMEM)
PARAMS = pltpu.CompilerParams(vmem_limit_bytes=48 * 1024 * 1024)


def homes():
    pairs = []
    for x in range(X):
        for y in range(Y):
            for core in range(CORES):
                for z in range(PANELS):
                    at, columns = UNITS[core, z % 3]
                    triple = (z - at) % PANELS // 3
                    user = 16 * triple + 2 * y + x % 2
                    column = (z + columns[x // 2]) % PANELS
                    source = ((x * Y + y) * CORES + core) * PANELS + z
                    pairs.append((source, user * PANELS + column))
    return pairs


def square_sum(panels):
    values = [panel.astype(jnp.float32) for panel in panels]
    return jnp.sum(sum(v * v for v in values), axis=1)


def per_device(ratings, counts):
    rows, width = CORES * ratings.shape[0], ratings.shape[1]
    x, y, core, me = (lax.axis_index(name) for name in ("x", "y", "core", "z"))
    place = jnp.stack([core, me % 3, 2 * y + x % 2]).astype(jnp.int32)

    def swap(array):
        return lax.ppermute(array, "core", [(0, 1), (1, 0)])

    def hop(array):
        return lax.ppermute(
            array,
            ("core", "z"),
            [
                (c * PANELS + z, c * PANELS + (z + (1 if c else -1)) % PANELS)
                for c in range(CORES)
                for z in range(PANELS)
            ],
        )

    both = jax.ShapeDtypeStruct((rows, width), ratings.dtype)
    own = pl.pallas_call(
        pair_kernel,
        out_shape=both,
        in_specs=[SMEM, VMEM, VMEM],
        out_specs=VMEM,
        compiler_params=PARAMS,
        name="pair",
    )(place, ratings, swap(ratings))
    ahead, behind = [own], []
    for step in range(HOPS):
        ahead.append(hop(ahead[-1]))
        if step == 0:
            later, ahead[1] = lax.optimization_barrier((counts, ahead[1]))
            other_counts = swap(later)
        if step < HOPS - 1:
            behind.append(swap(ahead[-1]))
    near = square_sum([ahead[0], ahead[1], ahead[2], behind[0]]).reshape(-1, 128)
    far = lax.ppermute(near, "z", [(z, (z + 6) % PANELS) for z in range(PANELS)])
    everything = jnp.concatenate([place, counts, other_counts])
    slots = jax.ShapeDtypeStruct((SLOTS, SLOT_ROWS, width), jnp.bfloat16)
    partial = pl.pallas_call(
        partial_kernel,
        out_shape=slots,
        in_specs=[SMEM] + [VMEM] * (2 + 2 * HOPS),
        out_specs=VMEM,
        scratch_shapes=[
            pltpu.VMEM((6 * width, width), jnp.float32),
            pltpu.VMEM((8, width), jnp.float32),
        ],
        compiler_params=PARAMS,
        name="partial",
    )(everything, near, far, *ahead, *behind)
    got = lax.all_to_all(partial, ("x", "y"), 0, 0, tiled=True)
    block = pl.pallas_call(
        finish_kernel,
        out_shape=jax.ShapeDtypeStruct((SHARE, width), jnp.bfloat16),
        in_specs=[SMEM, VMEM],
        out_specs=VMEM,
        compiler_params=PARAMS,
        name="finish",
    )(place, got)
    return lax.ppermute(block, ("x", "y", "core", "z"), homes())


def solution(mesh):
    fine = Mesh(mesh.devices.reshape(X, Y, CORES, PANELS), ("x", "y", "core", "z"))
    users = ("x", "y", "core")
    return jax.shard_map(
        per_device,
        mesh=fine,
        in_specs=(P(users, "z"), P(users)),
        out_specs=P(users, "z"),
        check_vma=False,
    )
```

```python
import jax
import jax.numpy as jnp
from jax import lax
from jax.experimental import pallas as pl
from jax.experimental.pallas import tpu as pltpu
from jax.sharding import Mesh, PartitionSpec as P

X, Y, CORES, PANELS = 4, 8, 2, 12
SLOTS = X * Y
BLOCK = 64
ITEMS = 3072
SHARE = 48
LANES = 128
SLOT_ROWS = 2 * SHARE + 8
CORE, RESIDUE, SLAB, COUNTS = 0, 1, 2, 3
COLUMNS = ((9, 10, 11), (7, 8, 6), (5, 3, 4))


def split_rows(total):
    high = total.astype(jnp.bfloat16).astype(jnp.float32)
    first = lax.broadcasted_iota(jnp.int32, total.shape, 0) < 4
    return jnp.where(first, high, total - high)


def join_rows(extra):
    return extra + pltpu.roll(extra, 4, 0)


def partial_kernel(place_ref, sums_ref, *refs):
    panels, (keep_ref, send_ref, gram_ref, row_ref, column_ref) = refs[:6], refs[6:]
    core, residue = place_ref[CORE], place_ref[RESIDUE]
    rows, width = panels[0].shape
    sums = sums_ref[0]
    for i in range(1, PANELS):
        sums = sums + sums_ref[i]
    corner = lax.broadcasted_iota(jnp.int32, (LANES, LANES), 0) == lax.broadcasted_iota(
        jnp.int32, (LANES, LANES), 1
    )
    square_sum = jnp.concatenate(
        [
            jnp.sum(jnp.where(corner, sums[i : i + 1], 0.0), axis=1, keepdims=True)
            for i in range(rows // LANES)
        ],
        axis=0,
    )
    position = lax.broadcasted_iota(jnp.int32, (BLOCK, 1), 0)
    live = jnp.concatenate(
        [
            (position < place_ref[COUNTS + i]).astype(jnp.float32)
            for i in range(rows // BLOCK)
        ],
        axis=0,
    )
    scale = live / jnp.sqrt(square_sum / ITEMS + 1e-05)

    weighted = []
    degrees = []
    for panel in panels:
        values = panel[...].astype(jnp.float32)
        one = (scale * values).astype(jnp.bfloat16)
        weighted.append(one)
        degrees.append(
            jnp.sum(values * one.astype(jnp.float32), axis=0, keepdims=True)
        )
    places = (residue, lax.rem(residue + 2, 3), lax.rem(residue + 1, 3))
    for panel, at, degree in zip(panels[:3], places, degrees[:3]):
        for half in range(2):
            row_ref[pl.ds(2 * at + half, 1), :] = degree[:, half * LANES : (half + 1) * LANES]
    for unit, column in enumerate((0, 3, 4, 5)):
        for half in range(2):
            column_ref[pl.ds(2 * unit + half, 1), :] = degrees[column][
                :, half * LANES : (half + 1) * LANES
            ]
        for panel, at in zip(panels[:3], places):
            start = pl.multiple_of((3 * unit + at) * width, width)
            gram_ref[pl.ds(start, width), :] = lax.dot_general(
                panel[...],
                weighted[column],
                (((0,), (0,)), ((), ())),
                preferred_element_type=jnp.float32,
            )
    for x in range(X):
        for y in range(Y):
            start = (2 * y + x % 2) * SHARE
            low, high = start // LANES, (start + SHARE - 1) // LANES
            for mine in (True, False):
                unit = 2 * (core if mine else 1 - core) + x // 2
                four = [column_ref[pl.ds(2 * unit + half, 1), :] for half in range(2)]
                four += [row_ref[pl.ds(i, 1), :] for i in (low, high)]
                extra = split_rows(jnp.concatenate(four + four, axis=0))
                first = pl.multiple_of(unit * 3 * width + start, 16)
                block = gram_ref[pl.ds(first, SHARE), :]
                whole = jnp.concatenate([block[:, :LANES], block[:, LANES:], extra], axis=0)
                ref = keep_ref if mine else send_ref
                ref[x * Y + y] = whole.astype(ref.dtype)


def add_kernel(keep_ref, got_ref, out_ref):
    for slot in range(SLOTS):
        total = keep_ref[slot] + got_ref[slot].astype(jnp.float32)
        extra = split_rows(join_rows(total[2 * SHARE :]))
        out_ref[slot] = jnp.concatenate([total[: 2 * SHARE], extra], axis=0).astype(
            jnp.bfloat16
        )


def finish_kernel(place_ref, got_ref, out_ref):
    offset = lax.rem(place_ref[SLAB] * SHARE, LANES)
    total = got_ref[0].astype(jnp.float32)
    for slot in range(1, SLOTS):
        total = total + got_ref[slot].astype(jnp.float32)
    extra = join_rows(total[2 * SHARE :])
    lane = lax.broadcasted_iota(jnp.int32, (SHARE, LANES), 1)
    row = lax.broadcasted_iota(jnp.int32, (SHARE, LANES), 0) + offset
    row_degree = jnp.sum(
        jnp.where(lane == row, extra[2:3], 0.0) + jnp.where(lane + LANES == row, extra[3:4], 0.0),
        axis=1,
        keepdims=True,
    )
    row_inverse = 1.0 / jnp.sqrt(row_degree)
    for half in range(2):
        block = total[half * SHARE : (half + 1) * SHARE]
        column_inverse = 1.0 / jnp.sqrt(extra[half : half + 1])
        out_ref[:, half * LANES : (half + 1) * LANES] = (
            block * row_inverse * column_inverse
        ).astype(jnp.bfloat16)


VMEM = pl.BlockSpec(memory_space=pltpu.VMEM)
SMEM = pl.BlockSpec(memory_space=pltpu.SMEM)
PARAMS = pltpu.CompilerParams(vmem_limit_bytes=48 * 1024 * 1024)


def homes():
    pairs = []
    for x in range(X):
        for y in range(Y):
            for core in range(CORES):
                for z in range(PANELS):
                    triple, residue = z // 3, z % 3
                    unit = 2 * core + x // 2
                    column = z
                    if unit:
                        column = (3 * triple + COLUMNS[residue][unit - 1]) % PANELS
                    user = 16 * triple + 2 * y + x % 2
                    source = ((x * Y + y) * CORES + core) * PANELS + z
                    pairs.append((source, user * PANELS + column))
    return pairs


def per_device(ratings, counts):
    rows, width = ratings.shape
    x, y, core, me = (lax.axis_index(name) for name in ("x", "y", "core", "z"))
    place = jnp.stack([core, me % 3, 2 * y + x % 2]).astype(jnp.int32)
    place = jnp.concatenate([place, counts])

    columns = [
        lax.ppermute(
            ratings,
            "z",
            [((z // 3 * 3 + COLUMNS[z % 3][i]) % PANELS, z) for z in range(PANELS)],
        )
        for i in range(3)
    ]
    triple = [ratings] + [
        lax.ppermute(
            ratings, "z", [(z // 3 * 3 + (z + by) % 3, z) for z in range(PANELS)]
        )
        for by in (2, 1)
    ]
    values = ratings.astype(jnp.float32)
    squares = jnp.sum(values * values, axis=1).reshape(rows // LANES, LANES)
    squares = jnp.pad(squares, ((0, 8 - rows // LANES), (0, 0)))
    squares = jnp.broadcast_to(squares[None], (PANELS, 8, LANES))
    squares = lax.all_to_all(squares, "z", 0, 0, tiled=True)

    slots = (SLOTS, SLOT_ROWS, LANES)
    keep, send = pl.pallas_call(
        partial_kernel,
        out_shape=(
            jax.ShapeDtypeStruct(slots, jnp.float32),
            jax.ShapeDtypeStruct(slots, jnp.bfloat16),
        ),
        in_specs=[SMEM] + [VMEM] * 7,
        out_specs=(VMEM, VMEM),
        scratch_shapes=[
            pltpu.VMEM((12 * width, width), jnp.float32),
            pltpu.VMEM((8, LANES), jnp.float32),
            pltpu.VMEM((8, LANES), jnp.float32),
        ],
        compiler_params=PARAMS,
        name="partial",
    )(place, squares, *triple, *columns)
    got = lax.ppermute(send, "core", [(0, 1), (1, 0)])
    total = pl.pallas_call(
        add_kernel,
        out_shape=jax.ShapeDtypeStruct(slots, jnp.bfloat16),
        in_specs=[VMEM, VMEM],
        out_specs=VMEM,
        compiler_params=PARAMS,
        name="add",
    )(keep, got)
    parts = lax.all_to_all(total, ("x", "y"), 0, 0, tiled=True)
    block = pl.pallas_call(
        finish_kernel,
        out_shape=jax.ShapeDtypeStruct((SHARE, width), jnp.bfloat16),
        in_specs=[SMEM, VMEM],
        out_specs=VMEM,
        compiler_params=PARAMS,
        name="finish",
    )(place, parts)
    return lax.ppermute(block, ("x", "y", "core", "z"), homes())


def solution(mesh):
    fine = Mesh(mesh.devices.reshape(X, Y, CORES, PANELS), ("x", "y", "core", "z"))
    users = ("x", "y", "core")
    return jax.shard_map(
        per_device,
        mesh=fine,
        in_specs=(P(users, "z"), P(users)),
        out_specs=P(users, "z"),
        check_vma=False,
    )
```

```python
import jax
import jax.numpy as jnp
from jax import lax
from jax.experimental import pallas as pl
from jax.experimental.pallas import tpu as pltpu
from jax.sharding import Mesh, PartitionSpec as P

X, Y, CORES, PANELS = 4, 8, 2, 12
SLOTS = X * Y
BLOCK = 64
ITEMS = 3072
SHARE = 48
LANES = 128
SLOT_ROWS = 2 * SHARE + 8
AXES = ("x", "y", "core", "triple", "member")
CORE, RESIDUE, SLAB, COUNTS = 0, 1, 2, 3
TRIPLES, MEMBERS = 4, 3
FAR = ((9, 10, 11), (5, 6, 8), (3, 4, 7))


def far_columns():
    wanted = []
    for z in range(PANELS):
        triple, member = divmod(z, MEMBERS)
        offsets = FAR[member]
        if triple % 2:
            offsets = [2 - offset for offset in FAR[2 - member]]
        wanted.append([(3 * triple + offset) % PANELS for offset in offsets])
    rounds = []
    for _ in range(3):
        taken = {}

        def place(z, seen):
            for panel in wanted[z]:
                if panel not in seen:
                    seen.add(panel)
                    if panel not in taken or place(taken[panel], seen):
                        taken[panel] = z
                        return True
            return False

        for z in range(PANELS):
            place(z, set())
        chosen = {z: panel for panel, z in taken.items()}
        rounds.append([chosen[z] for z in range(PANELS)])
        for z in range(PANELS):
            wanted[z].remove(chosen[z])
    return rounds


COLUMNS = far_columns()


def split_rows(total):
    high = total.astype(jnp.bfloat16).astype(jnp.float32)
    first = lax.broadcasted_iota(jnp.int32, total.shape, 0) < 4
    return jnp.where(first, high, total - high)


def join_rows(extra):
    return extra + pltpu.roll(extra, 4, 0)


def sums_kernel(ratings_ref, before_ref, after_ref, sums_ref, own_ref):
    own_ref[...] = ratings_ref[...]
    squares = jnp.zeros(ratings_ref.shape, jnp.float32)
    for ref in (ratings_ref, before_ref, after_ref):
        values = ref[...].astype(jnp.float32)
        squares = squares + values * values
    upright = jnp.sum(squares, axis=1, keepdims=True)
    corner = lax.broadcasted_iota(jnp.int32, (LANES, LANES), 0) == lax.broadcasted_iota(
        jnp.int32, (LANES, LANES), 1
    )
    lying = [
        jnp.sum(jnp.where(corner, upright[i : i + LANES], 0.0), axis=0, keepdims=True)
        for i in range(0, upright.shape[0], LANES)
    ]
    lying.append(jnp.zeros((8 - len(lying), LANES), jnp.float32))
    sums = jnp.concatenate(lying, axis=0)
    for i in range(TRIPLES):
        sums_ref[i] = sums


def partial_kernel(place_ref, sums_ref, *refs):
    panels, (keep_ref, send_ref, gram_ref, row_ref, column_ref) = refs[:6], refs[6:]
    core, residue = place_ref[CORE], place_ref[RESIDUE]
    rows, width = panels[0].shape
    sums = sums_ref[0]
    for i in range(1, TRIPLES):
        sums = sums + sums_ref[i]
    corner = lax.broadcasted_iota(jnp.int32, (LANES, LANES), 0) == lax.broadcasted_iota(
        jnp.int32, (LANES, LANES), 1
    )
    square_sum = jnp.concatenate(
        [
            jnp.sum(jnp.where(corner, sums[i : i + 1], 0.0), axis=1, keepdims=True)
            for i in range(rows // LANES)
        ],
        axis=0,
    )
    position = lax.broadcasted_iota(jnp.int32, (BLOCK, 1), 0)
    live = jnp.concatenate(
        [
            (position < place_ref[COUNTS + i]).astype(jnp.float32)
            for i in range(rows // BLOCK)
        ],
        axis=0,
    )
    scale = live / jnp.sqrt(square_sum / ITEMS + 1e-05)

    weighted = []
    degrees = []
    for panel in panels:
        values = panel[...].astype(jnp.float32)
        one = (scale * values).astype(jnp.bfloat16)
        weighted.append(one)
        degrees.append(
            jnp.sum(values * one.astype(jnp.float32), axis=0, keepdims=True)
        )
    places = (residue, lax.rem(residue + 2, 3), lax.rem(residue + 1, 3))
    for panel, at, degree in zip(panels[:3], places, degrees[:3]):
        for half in range(2):
            row_ref[pl.ds(2 * at + half, 1), :] = degree[:, half * LANES : (half + 1) * LANES]
    for unit, column in enumerate((0, 3, 4, 5)):
        for half in range(2):
            column_ref[pl.ds(2 * unit + half, 1), :] = degrees[column][
                :, half * LANES : (half + 1) * LANES
            ]
        for panel, at in zip(panels[:3], places):
            start = pl.multiple_of((3 * unit + at) * width, width)
            gram_ref[pl.ds(start, width), :] = lax.dot_general(
                panel[...],
                weighted[column],
                (((0,), (0,)), ((), ())),
                preferred_element_type=jnp.float32,
            )
    for x in range(X):
        for y in range(Y):
            start = (2 * y + x % 2) * SHARE
            low, high = start // LANES, (start + SHARE - 1) // LANES
            for mine in (True, False):
                unit = 2 * (core if mine else 1 - core) + x // 2
                four = [column_ref[pl.ds(2 * unit + half, 1), :] for half in range(2)]
                four += [row_ref[pl.ds(i, 1), :] for i in (low, high)]
                extra = split_rows(jnp.concatenate(four + four, axis=0))
                first = pl.multiple_of(unit * 3 * width + start, 16)
                block = gram_ref[pl.ds(first, SHARE), :]
                whole = jnp.concatenate([block[:, :LANES], block[:, LANES:], extra], axis=0)
                ref = keep_ref if mine else send_ref
                ref[x * Y + y] = whole.astype(ref.dtype)


def add_kernel(keep_ref, got_ref, out_ref):
    for slot in range(SLOTS):
        total = keep_ref[slot] + got_ref[slot].astype(jnp.float32)
        extra = split_rows(join_rows(total[2 * SHARE :]))
        out_ref[slot] = jnp.concatenate([total[: 2 * SHARE], extra], axis=0).astype(
            jnp.bfloat16
        )


def finish_kernel(place_ref, got_ref, out_ref):
    offset = lax.rem(place_ref[SLAB] * SHARE, LANES)
    total = got_ref[0].astype(jnp.float32)
    for slot in range(1, SLOTS):
        total = total + got_ref[slot].astype(jnp.float32)
    extra = join_rows(total[2 * SHARE :])
    lane = lax.broadcasted_iota(jnp.int32, (SHARE, LANES), 1)
    row = lax.broadcasted_iota(jnp.int32, (SHARE, LANES), 0) + offset
    row_degree = jnp.sum(
        jnp.where(lane == row, extra[2:3], 0.0) + jnp.where(lane + LANES == row, extra[3:4], 0.0),
        axis=1,
        keepdims=True,
    )
    row_inverse = 1.0 / jnp.sqrt(row_degree)
    for half in range(2):
        block = total[half * SHARE : (half + 1) * SHARE]
        column_inverse = 1.0 / jnp.sqrt(extra[half : half + 1])
        out_ref[:, half * LANES : (half + 1) * LANES] = (
            block * row_inverse * column_inverse
        ).astype(jnp.bfloat16)


VMEM = pl.BlockSpec(memory_space=pltpu.VMEM)
SMEM = pl.BlockSpec(memory_space=pltpu.SMEM)
PARAMS = pltpu.CompilerParams(vmem_limit_bytes=48 * 1024 * 1024)


def homes():
    pairs = []
    for x in range(X):
        for y in range(Y):
            for core in range(CORES):
                for z in range(PANELS):
                    unit = 2 * core + x // 2
                    column = COLUMNS[unit - 1][z] if unit else z
                    user = 16 * (z // MEMBERS) + 2 * y + x % 2
                    source = ((x * Y + y) * CORES + core) * PANELS + z
                    pairs.append((source, user * PANELS + column))
    return pairs


def per_device(ratings, counts):
    rows, width = ratings.shape
    x, y, core, member = (lax.axis_index(name) for name in ("x", "y", "core", "member"))
    place = jnp.stack([core, member, 2 * y + x % 2]).astype(jnp.int32)
    place = jnp.concatenate([place, counts])

    def fetch(sources):
        pairs = [(source, z) for z, source in enumerate(sources)]
        return lax.ppermute(ratings, ("triple", "member"), pairs)

    triple = [fetch([z // 3 * 3 + (z + by) % 3 for z in range(PANELS)]) for by in (2, 1)]
    columns = [fetch(sources) for sources in COLUMNS]
    sums, own = pl.pallas_call(
        sums_kernel,
        out_shape=(
            jax.ShapeDtypeStruct((TRIPLES, 8, LANES), jnp.float32),
            jax.ShapeDtypeStruct((rows, width), ratings.dtype),
        ),
        in_specs=[VMEM] * 3,
        out_specs=(VMEM, VMEM),
        compiler_params=PARAMS,
        name="sums",
    )(ratings, *triple)
    sums = lax.all_to_all(sums, "triple", 0, 0, tiled=True)

    slots = (SLOTS, SLOT_ROWS, LANES)
    keep, send = pl.pallas_call(
        partial_kernel,
        out_shape=(
            jax.ShapeDtypeStruct(slots, jnp.float32),
            jax.ShapeDtypeStruct(slots, jnp.bfloat16),
        ),
        in_specs=[SMEM] + [VMEM] * 7,
        out_specs=(VMEM, VMEM),
        scratch_shapes=[
            pltpu.VMEM((12 * width, width), jnp.float32),
            pltpu.VMEM((8, LANES), jnp.float32),
            pltpu.VMEM((8, LANES), jnp.float32),
        ],
        compiler_params=PARAMS,
        name="partial",
    )(place, sums, own, *triple, *columns)
    got = lax.ppermute(send, "core", [(0, 1), (1, 0)])
    total = pl.pallas_call(
        add_kernel,
        out_shape=jax.ShapeDtypeStruct(slots, jnp.bfloat16),
        in_specs=[VMEM, VMEM],
        out_specs=VMEM,
        compiler_params=PARAMS,
        name="add",
    )(keep, got)
    parts = lax.all_to_all(total, ("x", "y"), 0, 0, tiled=True)
    block = pl.pallas_call(
        finish_kernel,
        out_shape=jax.ShapeDtypeStruct((SHARE, width), jnp.bfloat16),
        in_specs=[SMEM, VMEM],
        out_specs=VMEM,
        compiler_params=PARAMS,
        name="finish",
    )(place, parts)
    return lax.ppermute(block, AXES, homes())


def solution(mesh):
    fine = Mesh(mesh.devices.reshape(X, Y, CORES, TRIPLES, MEMBERS), AXES)
    users, items = AXES[:3], AXES[3:]
    return jax.shard_map(
        per_device,
        mesh=fine,
        in_specs=(P(users, items), P(users)),
        out_specs=P(users, items),
        check_vma=False,
    )
```

```python
import jax
import jax.numpy as jnp
from jax import lax
from jax.experimental import pallas as pl
from jax.experimental.pallas import tpu as pltpu
from jax.sharding import Mesh, PartitionSpec as P

X, Y, CORES, PANELS = 4, 8, 2, 12
SLOTS = X * Y
BLOCK = 64
ITEMS = 3072
SHARE = 48
LANES = 128
SLOT_ROWS = 2 * SHARE + 8
AXES = ("x", "y", "core", "triple", "member")
COUNTS = 4
AXES = ("x", "y", "core", "z")
MEMBERS = 3
REACH = 3
UNITS = ((-3, (4, 1, 3, 2)), (-1, (2, 0, 1, -1)), (1, (-3, 0, -2, -1)))


def split_rows(total):
    high = total.astype(jnp.bfloat16).astype(jnp.float32)
    first = lax.broadcasted_iota(jnp.int32, total.shape, 0) < 4
    return jnp.where(first, high, total - high)


def join_rows(extra):
    return extra + pltpu.roll(extra, 4, 0)


def held(place_ref):
    member = lax.rem(place_ref[3], MEMBERS)
    first = sum(jnp.where(member == i, UNITS[i][0], 0) for i in range(MEMBERS))
    return member, lax.div(lax.rem(place_ref[3] + first + PANELS, PANELS), MEMBERS)


def diagonal():
    shape = (LANES, LANES)
    rows = lax.broadcasted_iota(jnp.int32, shape, 0)
    return rows == lax.broadcasted_iota(jnp.int32, shape, 1)


def sums_kernel(*refs):
    panels, (sums_ref, own_ref) = refs[:-2], refs[-2:]
    own_ref[...] = panels[0][...]
    squares = jnp.zeros(own_ref.shape, jnp.float32)
    for ref in panels:
        values = ref[...].astype(jnp.float32)
        squares = squares + values * values
    upright = jnp.sum(squares, axis=1, keepdims=True)
    corner = diagonal()
    lying = [
        jnp.sum(jnp.where(corner, upright[i : i + LANES], 0.0), axis=0, keepdims=True)
        for i in range(0, upright.shape[0], LANES)
    ]
    lying.append(jnp.zeros((8 - len(lying), LANES), jnp.float32))
    sums_ref[...] = jnp.concatenate(lying, axis=0)


def partial_kernel(place_ref, near_ref, far_ref, *refs):
    panels, (keep_ref, send_ref, gram_ref, row_ref, column_ref) = refs[:8], refs[8:]
    core = place_ref[2]
    member, triple = held(place_ref)
    rows, width = panels[0].shape
    squares = jnp.zeros((rows, width), jnp.float32)
    for ref in (panels[0], panels[2 * REACH]):
        values = ref[...].astype(jnp.float32)
        squares = squares + values * values
    sums = near_ref[...] + far_ref[...]
    corner = diagonal()
    square_sum = jnp.sum(squares, axis=1, keepdims=True) + jnp.concatenate(
        [
            jnp.sum(jnp.where(corner, sums[i : i + 1], 0.0), axis=1, keepdims=True)
            for i in range(rows // LANES)
        ],
        axis=0,
    )
    position = lax.broadcasted_iota(jnp.int32, (BLOCK, 1), 0)
    live = jnp.concatenate(
        [
            (position < place_ref[COUNTS + i]).astype(jnp.float32)
            for i in range(rows // BLOCK)
        ],
        axis=0,
    )
    scale = live / jnp.sqrt(square_sum / ITEMS + 1e-05)

    def degree(ref):
        values = ref[...].astype(jnp.float32)
        weighted = (scale * values).astype(jnp.bfloat16)
        total = values * weighted.astype(jnp.float32)
        return weighted, jnp.sum(total, axis=0, keepdims=True)

    def keep_degree(target, at, total):
        for half in range(2):
            lanes = total[:, half * LANES : (half + 1) * LANES]
            target[pl.ds(2 * at + half, 1), :] = lanes

    for its_member, (first, columns) in enumerate(UNITS):

        @pl.when(member == its_member)
        def _():
            row_panels = [panels[REACH + first + i] for i in range(MEMBERS)]
            for i, ref in enumerate(row_panels):
                keep_degree(row_ref, i, degree(ref)[1])
            for unit, offset in enumerate(columns):
                weighted, total = degree(panels[REACH + offset])
                keep_degree(column_ref, unit, total)
                for i, ref in enumerate(row_panels):
                    gram_ref[pl.ds((3 * unit + i) * width, width), :] = lax.dot_general(
                        ref[...],
                        weighted,
                        (((0,), (0,)), ((), ())),
                        preferred_element_type=jnp.float32,
                    )

    for x in range(X):
        slot = lax.rem(triple + x, X) * Y
        for y in range(Y):
            start = (2 * y + x % 2) * SHARE
            low, high = start // LANES, (start + SHARE - 1) // LANES
            for mine in (True, False):
                unit = 2 * (core if mine else 1 - core) + x // 2
                four = [column_ref[pl.ds(2 * unit + half, 1), :] for half in range(2)]
                four += [row_ref[pl.ds(i, 1), :] for i in (low, high)]
                extra = split_rows(jnp.concatenate(four + four, axis=0))
                at = pl.multiple_of(unit * 3 * width + start, 16)
                block = gram_ref[pl.ds(at, SHARE), :]
                whole = jnp.concatenate([block[:, :LANES], block[:, LANES:], extra], axis=0)
                ref = keep_ref if mine else send_ref
                ref[slot + y] = whole.astype(ref.dtype)


def add_kernel(keep_ref, got_ref, out_ref):
    for slot in range(SLOTS):
        total = keep_ref[slot] + got_ref[slot].astype(jnp.float32)
        extra = split_rows(join_rows(total[2 * SHARE :]))
        out_ref[slot] = jnp.concatenate([total[: 2 * SHARE], extra], axis=0).astype(
            jnp.bfloat16
        )


def finish_kernel(place_ref, got_ref, out_ref):
    by = lax.rem(place_ref[0] - held(place_ref)[1] + X, X)
    offset = lax.rem((2 * place_ref[1] + lax.rem(by, 2)) * SHARE, LANES)
    total = got_ref[0].astype(jnp.float32)
    for slot in range(1, SLOTS):
        total = total + got_ref[slot].astype(jnp.float32)
    extra = join_rows(total[2 * SHARE :])
    lane = lax.broadcasted_iota(jnp.int32, (SHARE, LANES), 1)
    row = lax.broadcasted_iota(jnp.int32, (SHARE, LANES), 0) + offset
    row_degree = jnp.sum(
        jnp.where(lane == row, extra[2:3], 0.0) + jnp.where(lane + LANES == row, extra[3:4], 0.0),
        axis=1,
        keepdims=True,
    )
    row_inverse = 1.0 / jnp.sqrt(row_degree)
    for half in range(2):
        block = total[half * SHARE : (half + 1) * SHARE]
        column_inverse = 1.0 / jnp.sqrt(extra[half : half + 1])
        out_ref[:, half * LANES : (half + 1) * LANES] = (
            block * row_inverse * column_inverse
        ).astype(jnp.bfloat16)


VMEM = pl.BlockSpec(memory_space=pltpu.VMEM)
SMEM = pl.BlockSpec(memory_space=pltpu.SMEM)
PARAMS = pltpu.CompilerParams(vmem_limit_bytes=48 * 1024 * 1024)


def homes():
    pairs = []
    for x in range(X):
        for y in range(Y):
            for core in range(CORES):
                for z in range(PANELS):
                    first, columns = UNITS[z % MEMBERS]
                    triple = (z + first) % PANELS // MEMBERS
                    by = (x - triple) % X
                    column = (z + columns[2 * core + by // 2]) % PANELS
                    user = 16 * triple + 2 * y + by % 2
                    source = ((x * Y + y) * CORES + core) * PANELS + z
                    pairs.append((source, user * PANELS + column))
    return pairs


def per_device(ratings, counts):
    rows, width = ratings.shape
    x, y, core, me = (lax.axis_index(name) for name in AXES)
    place = jnp.concatenate([jnp.stack([x, y, core, me]).astype(jnp.int32), counts])

    def fetch(array, by, at=range(PANELS)):
        return lax.ppermute(array, "z", [((z + by) % PANELS, z) for z in at])

    above, below = [ratings], [ratings]
    for _ in range(REACH):
        above.append(fetch(above[-1], 1))
        below.append(fetch(below[-1], -1))
    last = fetch(ratings, REACH + 1, range(0, PANELS, MEMBERS))
    near, own = pl.pallas_call(
        sums_kernel,
        out_shape=(
            jax.ShapeDtypeStruct((8, LANES), jnp.float32),
            jax.ShapeDtypeStruct((rows, width), ratings.dtype),
        ),
        in_specs=[VMEM] * 5,
        out_specs=(VMEM, VMEM),
        compiler_params=PARAMS,
        name="sums",
    )(*above[:3], *below[1:3])
    far = fetch(near, PANELS // 2)
    panels = below[:0:-1] + [own] + above[1:] + [last]

    slots = (SLOTS, SLOT_ROWS, LANES)
    keep, send = pl.pallas_call(
        partial_kernel,
        out_shape=(
            jax.ShapeDtypeStruct(slots, jnp.float32),
            jax.ShapeDtypeStruct(slots, jnp.bfloat16),
        ),
        in_specs=[SMEM] + [VMEM] * 10,
        out_specs=(VMEM, VMEM),
        scratch_shapes=[
            pltpu.VMEM((12 * width, width), jnp.float32),
            pltpu.VMEM((8, LANES), jnp.float32),
            pltpu.VMEM((8, LANES), jnp.float32),
        ],
        compiler_params=PARAMS,
        name="partial",
    )(place, near, far, *panels)
    got = lax.ppermute(send, "core", [(0, 1), (1, 0)])
    total = pl.pallas_call(
        add_kernel,
        out_shape=jax.ShapeDtypeStruct(slots, jnp.bfloat16),
        in_specs=[VMEM, VMEM],
        out_specs=VMEM,
        compiler_params=PARAMS,
        name="add",
    )(keep, got)
    parts = lax.all_to_all(total, ("x", "y"), 0, 0, tiled=True)
    block = pl.pallas_call(
        finish_kernel,
        out_shape=jax.ShapeDtypeStruct((SHARE, width), jnp.bfloat16),
        in_specs=[SMEM, VMEM],
        out_specs=VMEM,
        compiler_params=PARAMS,
        name="finish",
    )(place, parts)
    return lax.ppermute(block, AXES, homes())


def solution(mesh):
    fine = Mesh(mesh.devices.reshape(X, Y, CORES, PANELS), AXES)
    users = AXES[:3]
    return jax.shard_map(
        per_device,
        mesh=fine,
        in_specs=(P(users, "z"), P(users)),
        out_specs=P(users, "z"),
        check_vma=False,
    )
```

```python
import itertools

import jax
import jax.numpy as jnp
from jax import lax
from jax.experimental import pallas as pl
from jax.experimental.pallas import tpu as pltpu
from jax.sharding import Mesh, PartitionSpec as P

X, Y, CORES, PANELS = 4, 8, 2, 12
SLOTS = X * Y
BLOCK = 64
ITEMS = 3072
SHARE = 48
LANES = 128
SLOT_ROWS = 2 * SHARE + 8
AXES = ("x", "y", "core", "triple", "member")
COUNTS = 4
AXES = ("x", "y", "core", "z")
MEMBERS = 3
REACH = 3
UNITS = ((-3, (4, 1, 3, 2)), (-1, (2, 0, 1, -1)), (1, (-3, 0, -2, -1)))


def split_rows(total):
    high = total.astype(jnp.bfloat16).astype(jnp.float32)
    first = lax.broadcasted_iota(jnp.int32, total.shape, 0) < 4
    return jnp.where(first, high, total - high)


def join_rows(extra):
    return extra + pltpu.roll(extra, 4, 0)


def held(place_ref):
    member = lax.rem(place_ref[3], MEMBERS)
    first = sum(jnp.where(member == i, UNITS[i][0], 0) for i in range(MEMBERS))
    return member, lax.div(lax.rem(place_ref[3] + first + PANELS, PANELS), MEMBERS)


def diagonal():
    shape = (LANES, LANES)
    rows = lax.broadcasted_iota(jnp.int32, shape, 0)
    return rows == lax.broadcasted_iota(jnp.int32, shape, 1)


def own_kernel(place_ref, ratings_ref, own_ref, out_ref):
    own_ref[...] = ratings_ref[...]
    for i in range(place_ref.shape[0]):
        out_ref[i] = place_ref[i]


def sums_kernel(*refs):
    panels, sums_ref = refs[:-1], refs[-1]
    squares = jnp.zeros(panels[0].shape, jnp.float32)
    for ref in panels:
        values = ref[...].astype(jnp.float32)
        squares = squares + values * values
    upright = jnp.sum(squares, axis=1, keepdims=True)
    corner = diagonal()
    lying = [
        jnp.sum(jnp.where(corner, upright[i : i + LANES], 0.0), axis=0, keepdims=True)
        for i in range(0, upright.shape[0], LANES)
    ]
    lying.append(jnp.zeros((8 - len(lying), LANES), jnp.float32))
    sums_ref[...] = jnp.concatenate(lying, axis=0)


def partial_kernel(place_ref, near_ref, far_ref, *refs):
    panels, (keep_ref, send_ref, gram_ref, row_ref, column_ref) = refs[:8], refs[8:]
    core = place_ref[2]
    member, triple = held(place_ref)
    rows, width = panels[0].shape
    squares = jnp.zeros((rows, width), jnp.float32)
    for ref in (panels[0], panels[2 * REACH]):
        values = ref[...].astype(jnp.float32)
        squares = squares + values * values
    sums = near_ref[...] + far_ref[...]
    corner = diagonal()
    square_sum = jnp.sum(squares, axis=1, keepdims=True) + jnp.concatenate(
        [
            jnp.sum(jnp.where(corner, sums[i : i + 1], 0.0), axis=1, keepdims=True)
            for i in range(rows // LANES)
        ],
        axis=0,
    )
    position = lax.broadcasted_iota(jnp.int32, (BLOCK, 1), 0)
    live = jnp.concatenate(
        [
            (position < place_ref[COUNTS + i]).astype(jnp.float32)
            for i in range(rows // BLOCK)
        ],
        axis=0,
    )
    scale = live / jnp.sqrt(square_sum / ITEMS + 1e-05)

    def degree(ref):
        values = ref[...].astype(jnp.float32)
        weighted = (scale * values).astype(jnp.bfloat16)
        total = values * weighted.astype(jnp.float32)
        return weighted, jnp.sum(total, axis=0, keepdims=True)

    def keep_degree(target, at, total):
        for half in range(2):
            lanes = total[:, half * LANES : (half + 1) * LANES]
            target[pl.ds(2 * at + half, 1), :] = lanes

    for its_core, its_member in itertools.product(range(CORES), range(MEMBERS)):
        first, columns = UNITS[its_member]

        def panel(offset, its_core=its_core):
            if offset > REACH:
                return panels[-1]
            return panels[REACH - offset if its_core else REACH + offset]

        @pl.when((core == its_core) & (member == its_member))
        def _(first=first, columns=columns, panel=panel):
            row_panels = [panel(first + i) for i in range(MEMBERS)]
            for i, ref in enumerate(row_panels):
                keep_degree(row_ref, i, degree(ref)[1])
            for unit, offset in enumerate(columns):
                weighted, total = degree(panel(offset))
                keep_degree(column_ref, unit, total)
                for i, ref in enumerate(row_panels):
                    gram_ref[pl.ds((3 * unit + i) * width, width), :] = lax.dot_general(
                        ref[...],
                        weighted,
                        (((0,), (0,)), ((), ())),
                        preferred_element_type=jnp.float32,
                    )

    for x in range(X):
        slot = lax.rem(triple + x, X) * Y
        for y in range(Y):
            start = (2 * y + x % 2) * SHARE
            low, high = start // LANES, (start + SHARE - 1) // LANES
            for mine in (True, False):
                unit = 2 * (core if mine else 1 - core) + x // 2
                four = [column_ref[pl.ds(2 * unit + half, 1), :] for half in range(2)]
                four += [row_ref[pl.ds(i, 1), :] for i in (low, high)]
                extra = split_rows(jnp.concatenate(four + four, axis=0))
                at = pl.multiple_of(unit * 3 * width + start, 16)
                block = gram_ref[pl.ds(at, SHARE), :]
                whole = jnp.concatenate([block[:, :LANES], block[:, LANES:], extra], axis=0)
                ref = keep_ref if mine else send_ref
                ref[slot + y] = whole.astype(ref.dtype)


def add_kernel(keep_ref, got_ref, out_ref):
    for slot in range(SLOTS):
        total = keep_ref[slot] + got_ref[slot].astype(jnp.float32)
        extra = split_rows(join_rows(total[2 * SHARE :]))
        out_ref[slot] = jnp.concatenate([total[: 2 * SHARE], extra], axis=0).astype(
            jnp.bfloat16
        )


def finish_kernel(place_ref, got_ref, out_ref):
    by = lax.rem(place_ref[0] - held(place_ref)[1] + X, X)
    offset = lax.rem((2 * place_ref[1] + lax.rem(by, 2)) * SHARE, LANES)
    total = got_ref[0].astype(jnp.float32)
    for slot in range(1, SLOTS):
        total = total + got_ref[slot].astype(jnp.float32)
    extra = join_rows(total[2 * SHARE :])
    lane = lax.broadcasted_iota(jnp.int32, (SHARE, LANES), 1)
    row = lax.broadcasted_iota(jnp.int32, (SHARE, LANES), 0) + offset
    row_degree = jnp.sum(
        jnp.where(lane == row, extra[2:3], 0.0) + jnp.where(lane + LANES == row, extra[3:4], 0.0),
        axis=1,
        keepdims=True,
    )
    row_inverse = 1.0 / jnp.sqrt(row_degree)
    for half in range(2):
        block = total[half * SHARE : (half + 1) * SHARE]
        column_inverse = 1.0 / jnp.sqrt(extra[half : half + 1])
        out_ref[:, half * LANES : (half + 1) * LANES] = (
            block * row_inverse * column_inverse
        ).astype(jnp.bfloat16)


VMEM = pl.BlockSpec(memory_space=pltpu.VMEM)
SMEM = pl.BlockSpec(memory_space=pltpu.SMEM)
PARAMS = pltpu.CompilerParams(vmem_limit_bytes=48 * 1024 * 1024)


def homes():
    pairs = []
    for x in range(X):
        for y in range(Y):
            for core in range(CORES):
                for z in range(PANELS):
                    first, columns = UNITS[z % MEMBERS]
                    triple = (z + first) % PANELS // MEMBERS
                    by = (x - triple) % X
                    column = (z + columns[2 * core + by // 2]) % PANELS
                    user = 16 * triple + 2 * y + by % 2
                    source = ((x * Y + y) * CORES + core) * PANELS + z
                    pairs.append((source, user * PANELS + column))
    return pairs


def per_device(ratings, counts):
    rows, width = ratings.shape
    x, y, core, me = (lax.axis_index(name) for name in AXES)
    place = jnp.concatenate([jnp.stack([x, y, core, me]).astype(jnp.int32), counts])

    def fetch(array, by, at=range(PANELS)):
        return lax.ppermute(array, "z", [((z + by) % PANELS, z) for z in at])

    def relay(array, by):
        pairs = []
        for c in range(CORES):
            shift = -by if c else by
            pairs += [(c * PANELS + (z + shift) % PANELS, c * PANELS + z) for z in range(PANELS)]
        return lax.ppermute(array, ("core", "z"), pairs)

    first, second = [ratings], [ratings]
    own, place = pl.pallas_call(
        own_kernel,
        out_shape=(
            jax.ShapeDtypeStruct((rows, width), ratings.dtype),
            jax.ShapeDtypeStruct(place.shape, jnp.int32),
        ),
        in_specs=[SMEM, VMEM],
        out_specs=(VMEM, SMEM),
        compiler_params=PARAMS,
        name="own",
    )(place, ratings)
    for i in range(REACH):
        first.append(relay(first[-1], 1))
        second.append(relay(second[-1], -1))
        if i == 0:
            first[1], own, place = lax.optimization_barrier((first[1], own, place))
    last = fetch(ratings, REACH + 1, range(0, PANELS, MEMBERS))
    near = pl.pallas_call(
        sums_kernel,
        out_shape=jax.ShapeDtypeStruct((8, LANES), jnp.float32),
        in_specs=[VMEM] * 5,
        out_specs=VMEM,
        compiler_params=PARAMS,
        name="sums",
    )(own, *first[1:3], *second[1:3])
    far = fetch(near, PANELS // 2)
    panels = second[:0:-1] + [own] + first[1:] + [last]

    slots = (SLOTS, SLOT_ROWS, LANES)
    keep, send = pl.pallas_call(
        partial_kernel,
        out_shape=(
            jax.ShapeDtypeStruct(slots, jnp.float32),
            jax.ShapeDtypeStruct(slots, jnp.bfloat16),
        ),
        in_specs=[SMEM] + [VMEM] * 10,
        out_specs=(VMEM, VMEM),
        scratch_shapes=[
            pltpu.VMEM((12 * width, width), jnp.float32),
            pltpu.VMEM((8, LANES), jnp.float32),
            pltpu.VMEM((8, LANES), jnp.float32),
        ],
        compiler_params=PARAMS,
        name="partial",
    )(place, near, far, *panels)
    got = lax.ppermute(send, "core", [(0, 1), (1, 0)])
    total = pl.pallas_call(
        add_kernel,
        out_shape=jax.ShapeDtypeStruct(slots, jnp.bfloat16),
        in_specs=[VMEM, VMEM],
        out_specs=VMEM,
        compiler_params=PARAMS,
        name="add",
    )(keep, got)
    parts = lax.all_to_all(total, ("x", "y"), 0, 0, tiled=True)
    block = pl.pallas_call(
        finish_kernel,
        out_shape=jax.ShapeDtypeStruct((SHARE, width), jnp.bfloat16),
        in_specs=[SMEM, VMEM],
        out_specs=VMEM,
        compiler_params=PARAMS,
        name="finish",
    )(place, parts)
    return lax.ppermute(block, AXES, homes())


def solution(mesh):
    fine = Mesh(mesh.devices.reshape(X, Y, CORES, PANELS), AXES)
    users = AXES[:3]
    return jax.shard_map(
        per_device,
        mesh=fine,
        in_specs=(P(users, "z"), P(users)),
        out_specs=P(users, "z"),
        check_vma=False,
    )
```

```python
import jax
import jax.numpy as jnp
from jax import lax
from jax.experimental import pallas as pl
from jax.experimental.pallas import tpu as pltpu
from jax.sharding import Mesh, PartitionSpec as P

X, Y, CORES, PANELS = 4, 8, 2, 12
SLOTS = X * Y
BLOCK = 64
ITEMS = 3072
SHARE = 48
LANES = 128
SLOT_ROWS = 2 * SHARE + 8
AXES = ("x", "y", "core", "triple", "member")
COUNTS = 4
AXES = ("x", "y", "core", "z")
UP, DOWN = 6, 5


def split_rows(total):
    high = total.astype(jnp.bfloat16).astype(jnp.float32)
    first = lax.broadcasted_iota(jnp.int32, total.shape, 0) < 4
    return jnp.where(first, high, total - high)


def join_rows(extra):
    return extra + pltpu.roll(extra, 4, 0)


def partial_kernel(place_ref, *refs):
    panels, (keep_ref, send_ref, gram_ref, degree_ref) = refs[:PANELS], refs[PANELS:]
    core, me = place_ref[2], place_ref[3]
    rows, width = panels[0].shape
    squares = jnp.zeros((rows, width), jnp.float32)
    for panel in panels:
        values = panel[...].astype(jnp.float32)
        squares = squares + values * values
    square_sum = jnp.sum(squares, axis=1, keepdims=True)
    position = lax.broadcasted_iota(jnp.int32, (BLOCK, 1), 0)
    live = jnp.concatenate(
        [
            (position < place_ref[COUNTS + i]).astype(jnp.float32)
            for i in range(rows // BLOCK)
        ],
        axis=0,
    )
    scale = live / jnp.sqrt(square_sum / ITEMS + 1e-05)
    column = (scale * panels[0][...].astype(jnp.float32)).astype(jnp.bfloat16)
    hops = list(range(UP + 1)) + list(range(-1, -DOWN - 1, -1))
    for panel, hop in zip(panels, hops):
        owner = lax.rem(me + PANELS + jnp.where(core == 0, hop, -hop), PANELS)
        gram_ref[pl.ds(pl.multiple_of(owner * width, width), width), :] = lax.dot_general(
            panel[...], column, (((0,), (0,)), ((), ())), preferred_element_type=jnp.float32
        )
        values = panel[...].astype(jnp.float32)
        weighted = (scale * values).astype(jnp.bfloat16).astype(jnp.float32)
        degree = jnp.sum(values * weighted, axis=0, keepdims=True)
        for half in range(2):
            lanes = degree[:, half * LANES : (half + 1) * LANES]
            degree_ref[pl.ds(2 * owner + half, 1), :] = lanes

    for slot in range(SLOTS):
        for mine in (True, False):
            start = (2 * slot + (core if mine else 1 - core)) * SHARE
            low = lax.shift_right_logical(start, 7)
            high = lax.shift_right_logical(start + SHARE - 1, 7)
            four = [degree_ref[pl.ds(i, 1), :] for i in (2 * me, 2 * me + 1, low, high)]
            extra = split_rows(jnp.concatenate(four + four, axis=0))
            block = gram_ref[pl.ds(pl.multiple_of(start, 16), SHARE), :]
            whole = jnp.concatenate([block[:, :LANES], block[:, LANES:], extra], axis=0)
            ref = keep_ref if mine else send_ref
            ref[slot] = whole.astype(ref.dtype)


def add_kernel(keep_ref, got_ref, out_ref):
    for slot in range(SLOTS):
        total = keep_ref[slot] + got_ref[slot].astype(jnp.float32)
        extra = split_rows(join_rows(total[2 * SHARE :]))
        out_ref[slot] = jnp.concatenate([total[: 2 * SHARE], extra], axis=0).astype(
            jnp.bfloat16
        )


def finish_kernel(place_ref, got_ref, out_ref):
    user = (place_ref[0] * Y + place_ref[1]) * CORES + place_ref[2]
    offset = lax.rem(user * SHARE, LANES)
    total = got_ref[0].astype(jnp.float32)
    for slot in range(1, SLOTS):
        total = total + got_ref[slot].astype(jnp.float32)
    extra = join_rows(total[2 * SHARE :])
    lane = lax.broadcasted_iota(jnp.int32, (SHARE, LANES), 1)
    row = lax.broadcasted_iota(jnp.int32, (SHARE, LANES), 0) + offset
    row_degree = jnp.sum(
        jnp.where(lane == row, extra[2:3], 0.0) + jnp.where(lane + LANES == row, extra[3:4], 0.0),
        axis=1,
        keepdims=True,
    )
    row_inverse = 1.0 / jnp.sqrt(row_degree)
    for half in range(2):
        block = total[half * SHARE : (half + 1) * SHARE]
        column_inverse = 1.0 / jnp.sqrt(extra[half : half + 1])
        out_ref[:, half * LANES : (half + 1) * LANES] = (
            block * row_inverse * column_inverse
        ).astype(jnp.bfloat16)


VMEM = pl.BlockSpec(memory_space=pltpu.VMEM)
SMEM = pl.BlockSpec(memory_space=pltpu.SMEM)
PARAMS = pltpu.CompilerParams(vmem_limit_bytes=48 * 1024 * 1024)


def per_device(ratings, counts):
    rows, width = ratings.shape
    x, y, core, me = (lax.axis_index(name) for name in AXES)
    place = jnp.concatenate([jnp.stack([x, y, core, me]).astype(jnp.int32), counts])

    def relay(array, by):
        pairs = []
        for c in range(CORES):
            shift = -by if c else by
            pairs += [(c * PANELS + (z + shift) % PANELS, c * PANELS + z) for z in range(PANELS)]
        return lax.ppermute(array, ("core", "z"), pairs)

    first, second = [ratings], [ratings]
    for hop in range(UP):
        first.append(relay(first[-1], 1))
        if hop < DOWN:
            second.append(relay(second[-1], -1))
    panels = first + second[1:]

    slots = (SLOTS, SLOT_ROWS, LANES)
    keep, send = pl.pallas_call(
        partial_kernel,
        out_shape=(
            jax.ShapeDtypeStruct(slots, jnp.float32),
            jax.ShapeDtypeStruct(slots, jnp.bfloat16),
        ),
        in_specs=[SMEM] + [VMEM] * PANELS,
        out_specs=(VMEM, VMEM),
        scratch_shapes=[
            pltpu.VMEM((ITEMS, width), jnp.float32),
            pltpu.VMEM((ITEMS // LANES, LANES), jnp.float32),
        ],
        compiler_params=PARAMS,
        name="partial",
    )(place, *panels)
    got = lax.ppermute(send, "core", [(0, 1), (1, 0)])
    total = pl.pallas_call(
        add_kernel,
        out_shape=jax.ShapeDtypeStruct(slots, jnp.bfloat16),
        in_specs=[VMEM, VMEM],
        out_specs=VMEM,
        compiler_params=PARAMS,
        name="add",
    )(keep, got)
    parts = lax.all_to_all(total, ("x", "y"), 0, 0, tiled=True)
    return pl.pallas_call(
        finish_kernel,
        out_shape=jax.ShapeDtypeStruct((SHARE, width), jnp.bfloat16),
        in_specs=[SMEM, VMEM],
        out_specs=VMEM,
        compiler_params=PARAMS,
        name="finish",
    )(place, parts)


def solution(mesh):
    fine = Mesh(mesh.devices.reshape(X, Y, CORES, PANELS), AXES)
    users = AXES[:3]
    return jax.shard_map(
        per_device,
        mesh=fine,
        in_specs=(P(users, "z"), P(users)),
        out_specs=P(users, "z"),
        check_vma=False,
    )
```

```python
import jax
import jax.numpy as jnp
from jax import lax
from jax.experimental import pallas as pl
from jax.experimental.pallas import tpu as pltpu
from jax.sharding import Mesh, PartitionSpec as P

X, Y, CORES, PANELS = 4, 8, 2, 12
SLOTS = X * Y
BLOCK = 64
ITEMS = 3072
SHARE = 48
LANES = 128
SLOT_ROWS = 2 * SHARE + 8
AXES = ("x", "y", "core", "triple", "member")
CORE, RESIDUE, SLAB, TRIPLE, COUNTS = 0, 1, 2, 3, 4
TRIPLES, MEMBERS = 4, 3
FAR = ((9, 10, 11), (5, 6, 8), (3, 4, 7))


def far_columns():
    wanted = []
    for z in range(PANELS):
        triple, member = divmod(z, MEMBERS)
        offsets = FAR[member]
        if triple % 2:
            offsets = [2 - offset for offset in FAR[2 - member]]
        wanted.append([(3 * triple + offset) % PANELS for offset in offsets])
    rounds = []
    for _ in range(3):
        taken = {}

        def place(z, seen):
            for panel in wanted[z]:
                if panel not in seen:
                    seen.add(panel)
                    if panel not in taken or place(taken[panel], seen):
                        taken[panel] = z
                        return True
            return False

        for z in range(PANELS):
            place(z, set())
        chosen = {z: panel for panel, z in taken.items()}
        rounds.append([chosen[z] for z in range(PANELS)])
        for z in range(PANELS):
            wanted[z].remove(chosen[z])
    return rounds


COLUMNS = far_columns()


def split_rows(total):
    high = total.astype(jnp.bfloat16).astype(jnp.float32)
    first = lax.broadcasted_iota(jnp.int32, total.shape, 0) < 4
    return jnp.where(first, high, total - high)


def join_rows(extra):
    return extra + pltpu.roll(extra, 4, 0)


def sums_kernel(ratings_ref, sums_ref, own_ref):
    own_ref[...] = ratings_ref[...]
    values = ratings_ref[...].astype(jnp.float32)
    upright = jnp.sum(values * values, axis=1, keepdims=True)
    corner = lax.broadcasted_iota(jnp.int32, (LANES, LANES), 0) == lax.broadcasted_iota(
        jnp.int32, (LANES, LANES), 1
    )
    lying = [
        jnp.sum(jnp.where(corner, upright[i : i + LANES], 0.0), axis=0, keepdims=True)
        for i in range(0, upright.shape[0], LANES)
    ]
    lying.append(jnp.zeros((8 - len(lying), LANES), jnp.float32))
    sums = jnp.concatenate(lying, axis=0)
    for i in range(PANELS):
        sums_ref[i] = sums


def partial_kernel(place_ref, sums_ref, *refs):
    panels, (keep_ref, send_ref, gram_ref, row_ref, column_ref) = refs[:6], refs[6:]
    core, residue = place_ref[CORE], place_ref[RESIDUE]
    rows, width = panels[0].shape
    sums = sums_ref[0]
    for i in range(1, PANELS):
        sums = sums + sums_ref[i]
    corner = lax.broadcasted_iota(jnp.int32, (LANES, LANES), 0) == lax.broadcasted_iota(
        jnp.int32, (LANES, LANES), 1
    )
    square_sum = jnp.concatenate(
        [
            jnp.sum(jnp.where(corner, sums[i : i + 1], 0.0), axis=1, keepdims=True)
            for i in range(rows // LANES)
        ],
        axis=0,
    )
    position = lax.broadcasted_iota(jnp.int32, (BLOCK, 1), 0)
    live = jnp.concatenate(
        [
            (position < place_ref[COUNTS + i]).astype(jnp.float32)
            for i in range(rows // BLOCK)
        ],
        axis=0,
    )
    scale = live / jnp.sqrt(square_sum / ITEMS + 1e-05)

    weighted = []
    degrees = []
    for panel in panels:
        values = panel[...].astype(jnp.float32)
        one = (scale * values).astype(jnp.bfloat16)
        weighted.append(one)
        degrees.append(
            jnp.sum(values * one.astype(jnp.float32), axis=0, keepdims=True)
        )
    places = (residue, lax.rem(residue + 2, 3), lax.rem(residue + 1, 3))
    for panel, at, degree in zip(panels[:3], places, degrees[:3]):
        for half in range(2):
            row_ref[pl.ds(2 * at + half, 1), :] = degree[:, half * LANES : (half + 1) * LANES]
    for unit, column in enumerate((0, 3, 4, 5)):
        for half in range(2):
            column_ref[pl.ds(2 * unit + half, 1), :] = degrees[column][
                :, half * LANES : (half + 1) * LANES
            ]
        for panel, at in zip(panels[:3], places):
            start = pl.multiple_of((3 * unit + at) * width, width)
            gram_ref[pl.ds(start, width), :] = lax.dot_general(
                panel[...],
                weighted[column],
                (((0,), (0,)), ((), ())),
                preferred_element_type=jnp.float32,
            )
    for x in range(X):
        slot = lax.rem(place_ref[TRIPLE] + x, X) * Y
        for y in range(Y):
            start = (2 * y + x % 2) * SHARE
            low, high = start // LANES, (start + SHARE - 1) // LANES
            for mine in (True, False):
                unit = 2 * (core if mine else 1 - core) + 1 - x // 2
                four = [column_ref[pl.ds(2 * unit + half, 1), :] for half in range(2)]
                four += [row_ref[pl.ds(i, 1), :] for i in (low, high)]
                extra = split_rows(jnp.concatenate(four + four, axis=0))
                first = pl.multiple_of(unit * 3 * width + start, 16)
                block = gram_ref[pl.ds(first, SHARE), :]
                whole = jnp.concatenate([block[:, :LANES], block[:, LANES:], extra], axis=0)
                ref = keep_ref if mine else send_ref
                ref[slot + y] = whole.astype(ref.dtype)


def add_kernel(keep_ref, got_ref, out_ref):
    for slot in range(SLOTS):
        total = keep_ref[slot] + got_ref[slot].astype(jnp.float32)
        extra = split_rows(join_rows(total[2 * SHARE :]))
        out_ref[slot] = jnp.concatenate([total[: 2 * SHARE], extra], axis=0).astype(
            jnp.bfloat16
        )


def finish_kernel(place_ref, got_ref, out_ref):
    offset = lax.rem(place_ref[SLAB] * SHARE, LANES)
    total = got_ref[0].astype(jnp.float32)
    for slot in range(1, SLOTS):
        total = total + got_ref[slot].astype(jnp.float32)
    extra = join_rows(total[2 * SHARE :])
    lane = lax.broadcasted_iota(jnp.int32, (SHARE, LANES), 1)
    row = lax.broadcasted_iota(jnp.int32, (SHARE, LANES), 0) + offset
    row_degree = jnp.sum(
        jnp.where(lane == row, extra[2:3], 0.0) + jnp.where(lane + LANES == row, extra[3:4], 0.0),
        axis=1,
        keepdims=True,
    )
    row_inverse = 1.0 / jnp.sqrt(row_degree)
    for half in range(2):
        block = total[half * SHARE : (half + 1) * SHARE]
        column_inverse = 1.0 / jnp.sqrt(extra[half : half + 1])
        out_ref[:, half * LANES : (half + 1) * LANES] = (
            block * row_inverse * column_inverse
        ).astype(jnp.bfloat16)


VMEM = pl.BlockSpec(memory_space=pltpu.VMEM)
SMEM = pl.BlockSpec(memory_space=pltpu.SMEM)
PARAMS = pltpu.CompilerParams(vmem_limit_bytes=48 * 1024 * 1024)


def homes():
    pairs = []
    for x in range(X):
        for y in range(Y):
            for core in range(CORES):
                for z in range(PANELS):
                    by = (x - z // MEMBERS) % X
                    unit = 2 * core + 1 - by // 2
                    column = COLUMNS[unit - 1][z] if unit else z
                    user = 16 * (z // MEMBERS) + 2 * y + by % 2
                    source = ((x * Y + y) * CORES + core) * PANELS + z
                    pairs.append((source, user * PANELS + column))
    return pairs


def per_device(ratings, counts):
    rows, width = ratings.shape
    x, y, core, group, member = (lax.axis_index(name) for name in AXES)
    place = jnp.stack([core, member, 2 * y + (x + group) % 2, group]).astype(jnp.int32)
    place = jnp.concatenate([place, counts])

    def fetch(array, sources):
        pairs = [(source, z) for z, source in enumerate(sources)]
        return lax.ppermute(array, AXES[3:], pairs)

    columns = [fetch(ratings, sources) for sources in COLUMNS]
    sums, own = pl.pallas_call(
        sums_kernel,
        out_shape=(
            jax.ShapeDtypeStruct((PANELS, 8, LANES), jnp.float32),
            jax.ShapeDtypeStruct((rows, width), ratings.dtype),
        ),
        in_specs=[VMEM],
        out_specs=(VMEM, VMEM),
        compiler_params=PARAMS,
        name="sums",
    )(ratings)
    sums = lax.all_to_all(sums, AXES[3:], 0, 0, tiled=True)
    triple = [fetch(own, [z // 3 * 3 + (z + by) % 3 for z in range(PANELS)]) for by in (2, 1)]

    slots = (SLOTS, SLOT_ROWS, LANES)
    keep, send = pl.pallas_call(
        partial_kernel,
        out_shape=(
            jax.ShapeDtypeStruct(slots, jnp.float32),
            jax.ShapeDtypeStruct(slots, jnp.bfloat16),
        ),
        in_specs=[SMEM] + [VMEM] * 7,
        out_specs=(VMEM, VMEM),
        scratch_shapes=[
            pltpu.VMEM((12 * width, width), jnp.float32),
            pltpu.VMEM((8, LANES), jnp.float32),
            pltpu.VMEM((8, LANES), jnp.float32),
        ],
        compiler_params=PARAMS,
        name="partial",
    )(place, sums, own, *triple, *columns)
    got = lax.ppermute(send, "core", [(0, 1), (1, 0)])
    total = pl.pallas_call(
        add_kernel,
        out_shape=jax.ShapeDtypeStruct(slots, jnp.bfloat16),
        in_specs=[VMEM, VMEM],
        out_specs=VMEM,
        compiler_params=PARAMS,
        name="add",
    )(keep, got)
    parts = lax.all_to_all(total, ("x", "y"), 0, 0, tiled=True)
    block = pl.pallas_call(
        finish_kernel,
        out_shape=jax.ShapeDtypeStruct((SHARE, width), jnp.bfloat16),
        in_specs=[SMEM, VMEM],
        out_specs=VMEM,
        compiler_params=PARAMS,
        name="finish",
    )(place, parts)
    return lax.ppermute(block, AXES, homes())


def solution(mesh):
    fine = Mesh(mesh.devices.reshape(X, Y, CORES, TRIPLES, MEMBERS), AXES)
    users, items = AXES[:3], AXES[3:]
    return jax.shard_map(
        per_device,
        mesh=fine,
        in_specs=(P(users, items), P(users)),
        out_specs=P(users, items),
        check_vma=False,
    )
```

```python
import itertools

import jax
import jax.numpy as jnp
from jax import lax
from jax.experimental import pallas as pl
from jax.experimental.pallas import tpu as pltpu
from jax.sharding import Mesh, PartitionSpec as P

X, Y, CORES, PANELS = 4, 8, 2, 12
SLOTS = X * Y
BLOCK = 64
ITEMS = 3072
SHARE = 48
LANES = 128
SLOT_ROWS = 2 * SHARE + 8
AXES = ("x", "y", "core", "triple", "member")
COUNTS = 4
AXES = ("x", "y", "core", "z")
MEMBERS = 3
REACH = 3
UNITS = ((-3, (4, 1, 3, 2)), (-1, (2, 0, 1, -1)), (1, (-3, 0, -2, -1)))


def split_rows(total):
    high = total.astype(jnp.bfloat16).astype(jnp.float32)
    first = lax.broadcasted_iota(jnp.int32, total.shape, 0) < 4
    return jnp.where(first, high, total - high)


def join_rows(extra):
    return extra + pltpu.roll(extra, 4, 0)


def held(place_ref):
    member = lax.rem(place_ref[3], MEMBERS)
    first = sum(jnp.where(member == i, UNITS[i][0], 0) for i in range(MEMBERS))
    return member, lax.div(lax.rem(place_ref[3] + first + PANELS, PANELS), MEMBERS)


def diagonal():
    shape = (LANES, LANES)
    rows = lax.broadcasted_iota(jnp.int32, shape, 0)
    return rows == lax.broadcasted_iota(jnp.int32, shape, 1)


def sums_kernel(*refs):
    panels, (sums_ref, own_ref) = refs[:-2], refs[-2:]
    own_ref[...] = panels[0][...]
    squares = jnp.zeros(own_ref.shape, jnp.float32)
    for ref in panels:
        values = ref[...].astype(jnp.float32)
        squares = squares + values * values
    upright = jnp.sum(squares, axis=1, keepdims=True)
    corner = diagonal()
    lying = [
        jnp.sum(jnp.where(corner, upright[i : i + LANES], 0.0), axis=0, keepdims=True)
        for i in range(0, upright.shape[0], LANES)
    ]
    lying.append(jnp.zeros((8 - len(lying), LANES), jnp.float32))
    sums_ref[...] = jnp.concatenate(lying, axis=0)


def weigh(scale, ref):
    values = ref[...].astype(jnp.float32)
    return values, (scale * values).astype(jnp.bfloat16)


def half_products(place_ref, scale, panels, gram_ref, partner):
    core, (member, _) = place_ref[2], held(place_ref)
    width = panels[0].shape[1]
    for its_core, its_member in itertools.product(range(CORES), range(MEMBERS)):
        first, columns = UNITS[its_member]
        at = 2 * (1 - its_core if partner else its_core)

        @pl.when((core == its_core) & (member == its_member))
        def _(first=first, columns=columns[at : at + 2]):
            for unit, offset in enumerate(columns):
                weighted = weigh(scale, panels[REACH + offset])[1]
                for i in range(MEMBERS):
                    gram_ref[pl.ds((3 * unit + i) * width, width), :] = lax.dot_general(
                        panels[REACH + first + i][...],
                        weighted,
                        (((0,), (0,)), ((), ())),
                        preferred_element_type=jnp.float32,
                    )


def write_slots(place_ref, gram_ref, row_ref, column_ref, out_ref, partner):
    core, (_, triple) = place_ref[2], held(place_ref)
    width = gram_ref.shape[1]
    base = 2 * (1 - core if partner else core)
    for x in range(X):
        slot = lax.rem(triple + x, X) * Y
        for y in range(Y):
            start = (2 * y + x % 2) * SHARE
            low, high = start // LANES, (start + SHARE - 1) // LANES
            unit = x // 2
            four = [column_ref[pl.ds(2 * (base + unit) + half, 1), :] for half in range(2)]
            four += [row_ref[pl.ds(i, 1), :] for i in (low, high)]
            extra = split_rows(jnp.concatenate(four + four, axis=0))
            block = gram_ref[pl.ds(unit * 3 * width + start, SHARE), :]
            whole = jnp.concatenate([block[:, :LANES], block[:, LANES:], extra], axis=0)
            out_ref[slot + y] = whole.astype(out_ref.dtype)


def send_kernel(place_ref, near_ref, far_ref, *refs):
    panels, (send_ref, scale_ref, row_ref, column_ref, gram_ref) = refs[:8], refs[8:]
    member = held(place_ref)[0]
    rows, width = panels[0].shape
    squares = jnp.zeros((rows, width), jnp.float32)
    for ref in (panels[0], panels[2 * REACH]):
        values = ref[...].astype(jnp.float32)
        squares = squares + values * values
    sums = near_ref[...] + far_ref[...]
    corner = diagonal()
    square_sum = jnp.sum(squares, axis=1, keepdims=True) + jnp.concatenate(
        [
            jnp.sum(jnp.where(corner, sums[i : i + 1], 0.0), axis=1, keepdims=True)
            for i in range(rows // LANES)
        ],
        axis=0,
    )
    position = lax.broadcasted_iota(jnp.int32, (BLOCK, 1), 0)
    live = jnp.concatenate(
        [
            (position < place_ref[COUNTS + i]).astype(jnp.float32)
            for i in range(rows // BLOCK)
        ],
        axis=0,
    )
    scale = live / jnp.sqrt(square_sum / ITEMS + 1e-05)

    scale_ref[...] = scale

    def keep_degree(target, at, ref):
        values, weighted = weigh(scale, ref)
        total = jnp.sum(values * weighted.astype(jnp.float32), axis=0, keepdims=True)
        for half in range(2):
            lanes = total[:, half * LANES : (half + 1) * LANES]
            target[pl.ds(2 * at + half, 1), :] = lanes

    for its_member, (first, columns) in enumerate(UNITS):

        @pl.when(member == its_member)
        def _(first=first, columns=columns):
            for i in range(MEMBERS):
                keep_degree(row_ref, i, panels[REACH + first + i])
            for unit, offset in enumerate(columns):
                keep_degree(column_ref, unit, panels[REACH + offset])

    half_products(place_ref, scale, panels, gram_ref, True)
    write_slots(place_ref, gram_ref, row_ref, column_ref, send_ref, True)


def keep_kernel(place_ref, scale_ref, row_ref, column_ref, *refs):
    panels, (keep_ref, gram_ref) = refs[:8], refs[8:]
    half_products(place_ref, scale_ref[...], panels, gram_ref, False)
    write_slots(place_ref, gram_ref, row_ref, column_ref, keep_ref, False)


def add_kernel(keep_ref, got_ref, out_ref):
    for slot in range(SLOTS):
        total = keep_ref[slot] + got_ref[slot].astype(jnp.float32)
        extra = split_rows(join_rows(total[2 * SHARE :]))
        out_ref[slot] = jnp.concatenate([total[: 2 * SHARE], extra], axis=0).astype(
            jnp.bfloat16
        )


def finish_kernel(place_ref, got_ref, out_ref):
    by = lax.rem(place_ref[0] - held(place_ref)[1] + X, X)
    offset = lax.rem((2 * place_ref[1] + lax.rem(by, 2)) * SHARE, LANES)
    total = got_ref[0].astype(jnp.float32)
    for slot in range(1, SLOTS):
        total = total + got_ref[slot].astype(jnp.float32)
    extra = join_rows(total[2 * SHARE :])
    lane = lax.broadcasted_iota(jnp.int32, (SHARE, LANES), 1)
    row = lax.broadcasted_iota(jnp.int32, (SHARE, LANES), 0) + offset
    row_degree = jnp.sum(
        jnp.where(lane == row, extra[2:3], 0.0) + jnp.where(lane + LANES == row, extra[3:4], 0.0),
        axis=1,
        keepdims=True,
    )
    row_inverse = 1.0 / jnp.sqrt(row_degree)
    for half in range(2):
        block = total[half * SHARE : (half + 1) * SHARE]
        column_inverse = 1.0 / jnp.sqrt(extra[half : half + 1])
        out_ref[:, half * LANES : (half + 1) * LANES] = (
            block * row_inverse * column_inverse
        ).astype(jnp.bfloat16)


VMEM = pl.BlockSpec(memory_space=pltpu.VMEM)
SMEM = pl.BlockSpec(memory_space=pltpu.SMEM)
PARAMS = pltpu.CompilerParams(vmem_limit_bytes=48 * 1024 * 1024)


def homes():
    pairs = []
    for x in range(X):
        for y in range(Y):
            for core in range(CORES):
                for z in range(PANELS):
                    first, columns = UNITS[z % MEMBERS]
                    triple = (z + first) % PANELS // MEMBERS
                    by = (x - triple) % X
                    column = (z + columns[2 * core + by // 2]) % PANELS
                    user = 16 * triple + 2 * y + by % 2
                    source = ((x * Y + y) * CORES + core) * PANELS + z
                    pairs.append((source, user * PANELS + column))
    return pairs


def per_device(ratings, counts):
    rows, width = ratings.shape
    x, y, core, me = (lax.axis_index(name) for name in AXES)
    place = jnp.concatenate([jnp.stack([x, y, core, me]).astype(jnp.int32), counts])

    def fetch(array, by, at=range(PANELS)):
        return lax.ppermute(array, "z", [((z + by) % PANELS, z) for z in at])

    above, below = [ratings], [ratings]
    for _ in range(REACH):
        above.append(fetch(above[-1], 1))
        below.append(fetch(below[-1], -1))
    last = fetch(ratings, REACH + 1, range(0, PANELS, MEMBERS))
    near, own = pl.pallas_call(
        sums_kernel,
        out_shape=(
            jax.ShapeDtypeStruct((8, LANES), jnp.float32),
            jax.ShapeDtypeStruct((rows, width), ratings.dtype),
        ),
        in_specs=[VMEM] * 5,
        out_specs=(VMEM, VMEM),
        compiler_params=PARAMS,
        name="sums",
    )(*above[:3], *below[1:3])
    far = fetch(near, PANELS // 2)
    panels = below[:0:-1] + [own] + above[1:] + [last]

    slots = (SLOTS, SLOT_ROWS, LANES)
    lanes = jax.ShapeDtypeStruct((8, LANES), jnp.float32)
    gram = [pltpu.VMEM((6 * width, width), jnp.float32)]
    cost = pl.CostEstimate(
        flops=12 * rows * width * width, bytes_accessed=12 * rows * width, transcendentals=0
    )
    send, *known = pl.pallas_call(
        send_kernel,
        out_shape=(
            jax.ShapeDtypeStruct(slots, jnp.bfloat16),
            jax.ShapeDtypeStruct((rows, 1), jnp.float32),
            lanes,
            lanes,
        ),
        in_specs=[SMEM] + [VMEM] * 10,
        out_specs=(VMEM,) * 4,
        scratch_shapes=gram,
        compiler_params=PARAMS,
        cost_estimate=cost,
        name="send",
    )(place, near, far, *panels)
    got = lax.ppermute(send, "core", [(0, 1), (1, 0)])
    keep = pl.pallas_call(
        keep_kernel,
        out_shape=jax.ShapeDtypeStruct(slots, jnp.float32),
        in_specs=[SMEM] + [VMEM] * 11,
        out_specs=VMEM,
        scratch_shapes=gram,
        compiler_params=PARAMS,
        cost_estimate=cost,
        name="keep",
    )(place, *known, *panels)
    total = pl.pallas_call(
        add_kernel,
        out_shape=jax.ShapeDtypeStruct(slots, jnp.bfloat16),
        in_specs=[VMEM, VMEM],
        out_specs=VMEM,
        compiler_params=PARAMS,
        name="add",
    )(keep, got)
    parts = lax.all_to_all(total, ("x", "y"), 0, 0, tiled=True)
    block = pl.pallas_call(
        finish_kernel,
        out_shape=jax.ShapeDtypeStruct((SHARE, width), jnp.bfloat16),
        in_specs=[SMEM, VMEM],
        out_specs=VMEM,
        compiler_params=PARAMS,
        name="finish",
    )(place, parts)
    return lax.ppermute(block, AXES, homes())


def solution(mesh):
    fine = Mesh(mesh.devices.reshape(X, Y, CORES, PANELS), AXES)
    users = AXES[:3]
    return jax.shard_map(
        per_device,
        mesh=fine,
        in_specs=(P(users, "z"), P(users)),
        out_specs=P(users, "z"),
        check_vma=False,
    )
```

```python
import itertools

import jax
import jax.numpy as jnp
from jax import lax
from jax.experimental import pallas as pl
from jax.experimental.pallas import tpu as pltpu
from jax.sharding import Mesh, PartitionSpec as P

X, Y, CORES, PANELS = 4, 8, 2, 12
SLOTS = X * Y
BLOCK = 64
ITEMS = 3072
SHARE = 48
LANES = 128
SLOT_ROWS = 2 * SHARE + 8
AXES = ("x", "y", "core", "triple", "member")
COUNTS = 4
AXES = ("x", "y", "core", "z")
MEMBERS = 3
REACH = 3
UNITS = ((-3, (4, 1, 3, 2)), (-1, (2, 0, 1, -1)), (1, (-3, 0, -2, -1)))


def split_rows(total):
    high = total.astype(jnp.bfloat16).astype(jnp.float32)
    first = lax.broadcasted_iota(jnp.int32, total.shape, 0) < 4
    return jnp.where(first, high, total - high)


def join_rows(extra):
    return extra + pltpu.roll(extra, 4, 0)


def held(place_ref):
    member = lax.rem(place_ref[3], MEMBERS)
    first = sum(jnp.where(member == i, UNITS[i][0], 0) for i in range(MEMBERS))
    return member, lax.div(lax.rem(place_ref[3] + first + PANELS, PANELS), MEMBERS)


def diagonal():
    shape = (LANES, LANES)
    rows = lax.broadcasted_iota(jnp.int32, shape, 0)
    return rows == lax.broadcasted_iota(jnp.int32, shape, 1)


def sums_kernel(*refs):
    panels, (sums_ref, own_ref) = refs[:-2], refs[-2:]
    own_ref[...] = panels[0][...]
    squares = jnp.zeros(own_ref.shape, jnp.float32)
    for ref in panels:
        values = ref[...].astype(jnp.float32)
        squares = squares + values * values
    upright = jnp.sum(squares, axis=1, keepdims=True)
    corner = diagonal()
    lying = [
        jnp.sum(jnp.where(corner, upright[i : i + LANES], 0.0), axis=0, keepdims=True)
        for i in range(0, upright.shape[0], LANES)
    ]
    lying.append(jnp.zeros((8 - len(lying), LANES), jnp.float32))
    sums_ref[...] = jnp.concatenate(lying, axis=0)


def weigh(scale, ref):
    values = ref[...].astype(jnp.float32)
    return values, (scale * values).astype(jnp.bfloat16)


def half_products(place_ref, scale, panels, gram_ref, partner):
    core, (member, _) = place_ref[2], held(place_ref)
    width = panels[0].shape[1]
    for its_core, its_member in itertools.product(range(CORES), range(MEMBERS)):
        first, columns = UNITS[its_member]
        at = 2 * (1 - its_core if partner else its_core)

        @pl.when((core == its_core) & (member == its_member))
        def _(first=first, columns=columns[at : at + 2]):
            for unit, offset in enumerate(columns):
                weighted = weigh(scale, panels[REACH + offset])[1]
                for i in range(MEMBERS):
                    gram_ref[pl.ds((3 * unit + i) * width, width), :] = lax.dot_general(
                        panels[REACH + first + i][...],
                        weighted,
                        (((0,), (0,)), ((), ())),
                        preferred_element_type=jnp.float32,
                    )


def write_slots(place_ref, gram_ref, row_ref, column_ref, out_ref, partner):
    core, (_, triple) = place_ref[2], held(place_ref)
    width = gram_ref.shape[1]
    base = 2 * (1 - core if partner else core)
    for x in range(X):
        slot = lax.rem(triple + x, X) * Y
        for y in range(Y):
            start = (2 * y + x % 2) * SHARE
            low, high = start // LANES, (start + SHARE - 1) // LANES
            unit = x // 2
            four = [column_ref[pl.ds(2 * (base + unit) + half, 1), :] for half in range(2)]
            four += [row_ref[pl.ds(i, 1), :] for i in (low, high)]
            extra = split_rows(jnp.concatenate(four + four, axis=0))
            block = gram_ref[pl.ds(unit * 3 * width + start, SHARE), :]
            whole = jnp.concatenate([block[:, :LANES], block[:, LANES:], extra], axis=0)
            out_ref[slot + y] = whole.astype(out_ref.dtype)


def send_kernel(place_ref, near_ref, far_ref, *refs):
    panels, (send_ref, scale_ref, row_ref, column_ref, gram_ref) = refs[:8], refs[8:]
    member = held(place_ref)[0]
    rows, width = panels[0].shape
    squares = jnp.zeros((rows, width), jnp.float32)
    for ref in (panels[0], panels[2 * REACH]):
        values = ref[...].astype(jnp.float32)
        squares = squares + values * values
    sums = near_ref[...] + far_ref[...]
    corner = diagonal()
    square_sum = jnp.sum(squares, axis=1, keepdims=True) + jnp.concatenate(
        [
            jnp.sum(jnp.where(corner, sums[i : i + 1], 0.0), axis=1, keepdims=True)
            for i in range(rows // LANES)
        ],
        axis=0,
    )
    position = lax.broadcasted_iota(jnp.int32, (BLOCK, 1), 0)
    live = jnp.concatenate(
        [
            (position < place_ref[COUNTS + i]).astype(jnp.float32)
            for i in range(rows // BLOCK)
        ],
        axis=0,
    )
    scale = live / jnp.sqrt(square_sum / ITEMS + 1e-05)

    scale_ref[...] = scale

    def keep_degree(target, at, ref):
        values, weighted = weigh(scale, ref)
        total = jnp.sum(values * weighted.astype(jnp.float32), axis=0, keepdims=True)
        for half in range(2):
            lanes = total[:, half * LANES : (half + 1) * LANES]
            target[pl.ds(2 * at + half, 1), :] = lanes

    for its_member, (first, columns) in enumerate(UNITS):

        @pl.when(member == its_member)
        def _(first=first, columns=columns):
            for i in range(MEMBERS):
                keep_degree(row_ref, i, panels[REACH + first + i])
            for unit, offset in enumerate(columns):
                keep_degree(column_ref, unit, panels[REACH + offset])

    half_products(place_ref, scale, panels, gram_ref, True)
    write_slots(place_ref, gram_ref, row_ref, column_ref, send_ref, True)


def keep_kernel(place_ref, scale_ref, row_ref, column_ref, *refs):
    panels, (keep_ref, gram_ref) = refs[:8], refs[8:]
    half_products(place_ref, scale_ref[...], panels, gram_ref, False)
    write_slots(place_ref, gram_ref, row_ref, column_ref, keep_ref, False)


def add_kernel(keep_ref, got_ref, out_ref):
    for slot in range(SLOTS):
        total = keep_ref[slot] + got_ref[slot].astype(jnp.float32)
        extra = split_rows(join_rows(total[2 * SHARE :]))
        out_ref[slot] = jnp.concatenate([total[: 2 * SHARE], extra], axis=0).astype(
            jnp.bfloat16
        )


def fold_kernel(got_ref, out_ref):
    for slot in range(Y):
        total = got_ref[slot].astype(jnp.float32)
        for x in range(1, X):
            total = total + got_ref[x * Y + slot].astype(jnp.float32)
        extra = split_rows(join_rows(total[2 * SHARE :]))
        out_ref[slot] = jnp.concatenate([total[: 2 * SHARE], extra], axis=0).astype(
            jnp.bfloat16
        )


def finish_kernel(place_ref, got_ref, out_ref):
    by = lax.rem(place_ref[0] - held(place_ref)[1] + X, X)
    offset = lax.rem((2 * place_ref[1] + lax.rem(by, 2)) * SHARE, LANES)
    total = got_ref[0].astype(jnp.float32)
    for slot in range(1, Y):
        total = total + got_ref[slot].astype(jnp.float32)
    extra = join_rows(total[2 * SHARE :])
    lane = lax.broadcasted_iota(jnp.int32, (SHARE, LANES), 1)
    row = lax.broadcasted_iota(jnp.int32, (SHARE, LANES), 0) + offset
    row_degree = jnp.sum(
        jnp.where(lane == row, extra[2:3], 0.0) + jnp.where(lane + LANES == row, extra[3:4], 0.0),
        axis=1,
        keepdims=True,
    )
    row_inverse = 1.0 / jnp.sqrt(row_degree)
    for half in range(2):
        block = total[half * SHARE : (half + 1) * SHARE]
        column_inverse = 1.0 / jnp.sqrt(extra[half : half + 1])
        out_ref[:, half * LANES : (half + 1) * LANES] = (
            block * row_inverse * column_inverse
        ).astype(jnp.bfloat16)


VMEM = pl.BlockSpec(memory_space=pltpu.VMEM)
SMEM = pl.BlockSpec(memory_space=pltpu.SMEM)
PARAMS = pltpu.CompilerParams(vmem_limit_bytes=48 * 1024 * 1024)


def homes():
    pairs = []
    for x in range(X):
        for y in range(Y):
            for core in range(CORES):
                for z in range(PANELS):
                    first, columns = UNITS[z % MEMBERS]
                    triple = (z + first) % PANELS // MEMBERS
                    by = (x - triple) % X
                    column = (z + columns[2 * core + by // 2]) % PANELS
                    user = 16 * triple + 2 * y + by % 2
                    source = ((x * Y + y) * CORES + core) * PANELS + z
                    pairs.append((source, user * PANELS + column))
    return pairs


def per_device(ratings, counts):
    rows, width = ratings.shape
    x, y, core, me = (lax.axis_index(name) for name in AXES)
    place = jnp.concatenate([jnp.stack([x, y, core, me]).astype(jnp.int32), counts])

    def fetch(array, by, at=range(PANELS)):
        return lax.ppermute(array, "z", [((z + by) % PANELS, z) for z in at])

    above, below = [ratings], [ratings]
    for _ in range(REACH):
        above.append(fetch(above[-1], 1))
        below.append(fetch(below[-1], -1))
    last = fetch(ratings, REACH + 1, range(0, PANELS, MEMBERS))
    near, own = pl.pallas_call(
        sums_kernel,
        out_shape=(
            jax.ShapeDtypeStruct((8, LANES), jnp.float32),
            jax.ShapeDtypeStruct((rows, width), ratings.dtype),
        ),
        in_specs=[VMEM] * 5,
        out_specs=(VMEM, VMEM),
        compiler_params=PARAMS,
        name="sums",
    )(*above[:3], *below[1:3])
    far = fetch(near, PANELS // 2)
    panels = below[:0:-1] + [own] + above[1:] + [last]

    slots = (SLOTS, SLOT_ROWS, LANES)
    lanes = jax.ShapeDtypeStruct((8, LANES), jnp.float32)
    gram = [pltpu.VMEM((6 * width, width), jnp.float32)]
    cost = pl.CostEstimate(
        flops=12 * rows * width * width, bytes_accessed=12 * rows * width, transcendentals=0
    )
    send, *known = pl.pallas_call(
        send_kernel,
        out_shape=(
            jax.ShapeDtypeStruct(slots, jnp.bfloat16),
            jax.ShapeDtypeStruct((rows, 1), jnp.float32),
            lanes,
            lanes,
        ),
        in_specs=[SMEM] + [VMEM] * 10,
        out_specs=(VMEM,) * 4,
        scratch_shapes=gram,
        compiler_params=PARAMS,
        cost_estimate=cost,
        name="send",
    )(place, near, far, *panels)
    got = lax.ppermute(send, "core", [(0, 1), (1, 0)])
    keep = pl.pallas_call(
        keep_kernel,
        out_shape=jax.ShapeDtypeStruct(slots, jnp.float32),
        in_specs=[SMEM] + [VMEM] * 11,
        out_specs=VMEM,
        scratch_shapes=gram,
        compiler_params=PARAMS,
        cost_estimate=cost,
        name="keep",
    )(place, *known, *panels)
    total = pl.pallas_call(
        add_kernel,
        out_shape=jax.ShapeDtypeStruct(slots, jnp.bfloat16),
        in_specs=[VMEM, VMEM],
        out_specs=VMEM,
        compiler_params=PARAMS,
        name="add",
    )(keep, got)
    parts = lax.all_to_all(total, "x", 0, 0, tiled=True)
    total = pl.pallas_call(
        fold_kernel,
        out_shape=jax.ShapeDtypeStruct((Y, SLOT_ROWS, LANES), jnp.bfloat16),
        in_specs=[VMEM],
        out_specs=VMEM,
        compiler_params=PARAMS,
        name="fold",
    )(parts)
    parts = lax.all_to_all(total, "y", 0, 0, tiled=True)
    block = pl.pallas_call(
        finish_kernel,
        out_shape=jax.ShapeDtypeStruct((SHARE, width), jnp.bfloat16),
        in_specs=[SMEM, VMEM],
        out_specs=VMEM,
        compiler_params=PARAMS,
        name="finish",
    )(place, parts)
    return lax.ppermute(block, AXES, homes())


def solution(mesh):
    fine = Mesh(mesh.devices.reshape(X, Y, CORES, PANELS), AXES)
    users = AXES[:3]
    return jax.shard_map(
        per_device,
        mesh=fine,
        in_specs=(P(users, "z"), P(users)),
        out_specs=P(users, "z"),
        check_vma=False,
    )
```

```python
import itertools

import jax
import jax.numpy as jnp
from jax import lax
from jax.experimental import pallas as pl
from jax.experimental.pallas import tpu as pltpu
from jax.sharding import Mesh, PartitionSpec as P

X, Y, CORES, PANELS = 4, 8, 2, 12
SLOTS = X * Y
BLOCK = 64
ITEMS = 3072
SHARE = 48
LANES = 128
SLOT_ROWS = 2 * SHARE + 8
AXES = ("x", "y", "core", "triple", "member")
COUNTS = 4
AXES = ("x", "y", "core", "z")
MEMBERS = 3
REACH = 3
UNITS = ((-3, (4, 1, 3, 2)), (-1, (2, 0, 1, -1)), (1, (-3, 0, -2, -1)))


def split_rows(total):
    high = total.astype(jnp.bfloat16).astype(jnp.float32)
    first = lax.broadcasted_iota(jnp.int32, total.shape, 0) < 4
    return jnp.where(first, high, total - high)


def join_rows(extra):
    return extra + pltpu.roll(extra, 4, 0)


def held(place_ref):
    member = lax.rem(place_ref[3], MEMBERS)
    first = sum(jnp.where(member == i, UNITS[i][0], 0) for i in range(MEMBERS))
    return member, lax.div(lax.rem(place_ref[3] + first + PANELS, PANELS), MEMBERS)


def diagonal():
    shape = (LANES, LANES)
    rows = lax.broadcasted_iota(jnp.int32, shape, 0)
    return rows == lax.broadcasted_iota(jnp.int32, shape, 1)


def sums_kernel(*refs):
    panels, (sums_ref, own_ref) = refs[:-2], refs[-2:]
    own_ref[...] = panels[0][...]
    squares = jnp.zeros(own_ref.shape, jnp.float32)
    for ref in panels:
        values = ref[...].astype(jnp.float32)
        squares = squares + values * values
    upright = jnp.sum(squares, axis=1, keepdims=True)
    corner = diagonal()
    lying = [
        jnp.sum(jnp.where(corner, upright[i : i + LANES], 0.0), axis=0, keepdims=True)
        for i in range(0, upright.shape[0], LANES)
    ]
    lying.append(jnp.zeros((8 - len(lying), LANES), jnp.float32))
    sums_ref[...] = jnp.concatenate(lying, axis=0)


def weigh(scale, ref):
    values = ref[...].astype(jnp.float32)
    return values, (scale * values).astype(jnp.bfloat16)


def panel_at(panels, core, offset):
    if offset > REACH:
        return panels[-1]
    return panels[REACH - offset if core else REACH + offset]


def half_products(place_ref, scale, panels, gram_ref, partner):
    core, (member, _) = place_ref[2], held(place_ref)
    width = panels[0].shape[1]
    for its_core, its_member in itertools.product(range(CORES), range(MEMBERS)):
        first, columns = UNITS[its_member]
        at = 2 * (1 - its_core if partner else its_core)

        @pl.when((core == its_core) & (member == its_member))
        def _(its_core=its_core, first=first, columns=columns[at : at + 2]):
            for unit, offset in enumerate(columns):
                weighted = weigh(scale, panel_at(panels, its_core, offset))[1]
                for i in range(MEMBERS):
                    gram_ref[pl.ds((3 * unit + i) * width, width), :] = lax.dot_general(
                        panel_at(panels, its_core, first + i)[...],
                        weighted,
                        (((0,), (0,)), ((), ())),
                        preferred_element_type=jnp.float32,
                    )


def write_slots(place_ref, gram_ref, row_ref, column_ref, out_ref, partner):
    core, (_, triple) = place_ref[2], held(place_ref)
    width = gram_ref.shape[1]
    base = 2 * (1 - core if partner else core)
    for x in range(X):
        slot = lax.rem(triple + x, X) * Y
        for y in range(Y):
            start = (2 * y + x % 2) * SHARE
            low, high = start // LANES, (start + SHARE - 1) // LANES
            unit = x // 2
            four = [column_ref[pl.ds(2 * (base + unit) + half, 1), :] for half in range(2)]
            four += [row_ref[pl.ds(i, 1), :] for i in (low, high)]
            extra = split_rows(jnp.concatenate(four + four, axis=0))
            block = gram_ref[pl.ds(unit * 3 * width + start, SHARE), :]
            whole = jnp.concatenate([block[:, :LANES], block[:, LANES:], extra], axis=0)
            out_ref[slot + y] = whole.astype(out_ref.dtype)


def send_kernel(place_ref, near_ref, far_ref, *refs):
    panels, (send_ref, scale_ref, row_ref, column_ref, gram_ref) = refs[:8], refs[8:]
    core, (member, _) = place_ref[2], held(place_ref)
    rows, width = panels[0].shape
    squares = jnp.zeros((rows, width), jnp.float32)
    for ref in (panels[0], panels[2 * REACH]):
        values = ref[...].astype(jnp.float32)
        squares = squares + values * values
    sums = near_ref[...] + far_ref[...]
    corner = diagonal()
    square_sum = jnp.sum(squares, axis=1, keepdims=True) + jnp.concatenate(
        [
            jnp.sum(jnp.where(corner, sums[i : i + 1], 0.0), axis=1, keepdims=True)
            for i in range(rows // LANES)
        ],
        axis=0,
    )
    position = lax.broadcasted_iota(jnp.int32, (BLOCK, 1), 0)
    live = jnp.concatenate(
        [
            (position < place_ref[COUNTS + i]).astype(jnp.float32)
            for i in range(rows // BLOCK)
        ],
        axis=0,
    )
    scale = live / jnp.sqrt(square_sum / ITEMS + 1e-05)

    scale_ref[...] = scale

    def keep_degree(target, at, ref):
        values, weighted = weigh(scale, ref)
        total = jnp.sum(values * weighted.astype(jnp.float32), axis=0, keepdims=True)
        for half in range(2):
            lanes = total[:, half * LANES : (half + 1) * LANES]
            target[pl.ds(2 * at + half, 1), :] = lanes

    for its_core, its_member in itertools.product(range(CORES), range(MEMBERS)):
        first, columns = UNITS[its_member]

        @pl.when((core == its_core) & (member == its_member))
        def _(its_core=its_core, first=first, columns=columns):
            for i in range(MEMBERS):
                keep_degree(row_ref, i, panel_at(panels, its_core, first + i))
            for unit, offset in enumerate(columns):
                keep_degree(column_ref, unit, panel_at(panels, its_core, offset))

    half_products(place_ref, scale, panels, gram_ref, True)
    write_slots(place_ref, gram_ref, row_ref, column_ref, send_ref, True)


def keep_kernel(place_ref, scale_ref, row_ref, column_ref, *refs):
    panels, (keep_ref, gram_ref) = refs[:8], refs[8:]
    half_products(place_ref, scale_ref[...], panels, gram_ref, False)
    write_slots(place_ref, gram_ref, row_ref, column_ref, keep_ref, False)


def add_kernel(keep_ref, got_ref, out_ref):
    for slot in range(SLOTS):
        total = keep_ref[slot] + got_ref[slot].astype(jnp.float32)
        extra = split_rows(join_rows(total[2 * SHARE :]))
        out_ref[slot] = jnp.concatenate([total[: 2 * SHARE], extra], axis=0).astype(
            jnp.bfloat16
        )


def fold_kernel(got_ref, out_ref):
    for slot in range(Y):
        total = got_ref[slot].astype(jnp.float32)
        for x in range(1, X):
            total = total + got_ref[x * Y + slot].astype(jnp.float32)
        extra = split_rows(join_rows(total[2 * SHARE :]))
        out_ref[slot] = jnp.concatenate([total[: 2 * SHARE], extra], axis=0).astype(
            jnp.bfloat16
        )


def finish_kernel(place_ref, got_ref, out_ref):
    by = lax.rem(place_ref[0] - held(place_ref)[1] + X, X)
    offset = lax.rem((2 * place_ref[1] + lax.rem(by, 2)) * SHARE, LANES)
    total = got_ref[0].astype(jnp.float32)
    for slot in range(1, Y):
        total = total + got_ref[slot].astype(jnp.float32)
    extra = join_rows(total[2 * SHARE :])
    lane = lax.broadcasted_iota(jnp.int32, (SHARE, LANES), 1)
    row = lax.broadcasted_iota(jnp.int32, (SHARE, LANES), 0) + offset
    row_degree = jnp.sum(
        jnp.where(lane == row, extra[2:3], 0.0) + jnp.where(lane + LANES == row, extra[3:4], 0.0),
        axis=1,
        keepdims=True,
    )
    row_inverse = 1.0 / jnp.sqrt(row_degree)
    for half in range(2):
        block = total[half * SHARE : (half + 1) * SHARE]
        column_inverse = 1.0 / jnp.sqrt(extra[half : half + 1])
        out_ref[:, half * LANES : (half + 1) * LANES] = (
            block * row_inverse * column_inverse
        ).astype(jnp.bfloat16)


VMEM = pl.BlockSpec(memory_space=pltpu.VMEM)
SMEM = pl.BlockSpec(memory_space=pltpu.SMEM)
PARAMS = pltpu.CompilerParams(vmem_limit_bytes=48 * 1024 * 1024)


def homes():
    pairs = []
    for x in range(X):
        for y in range(Y):
            for core in range(CORES):
                for z in range(PANELS):
                    first, columns = UNITS[z % MEMBERS]
                    triple = (z + first) % PANELS // MEMBERS
                    by = (x - triple) % X
                    column = (z + columns[2 * core + by // 2]) % PANELS
                    user = 16 * triple + 2 * y + by % 2
                    source = ((x * Y + y) * CORES + core) * PANELS + z
                    pairs.append((source, user * PANELS + column))
    return pairs


def per_device(ratings, counts):
    rows, width = ratings.shape
    x, y, core, me = (lax.axis_index(name) for name in AXES)
    place = jnp.concatenate([jnp.stack([x, y, core, me]).astype(jnp.int32), counts])

    def fetch(array, by, at=range(PANELS)):
        return lax.ppermute(array, "z", [((z + by) % PANELS, z) for z in at])

    def relay(array, by):
        pairs = []
        for c in range(CORES):
            shift = -by if c else by
            pairs += [(c * PANELS + (z + shift) % PANELS, c * PANELS + z) for z in range(PANELS)]
        return lax.ppermute(array, ("core", "z"), pairs)

    above, below = [ratings], [ratings]
    for _ in range(REACH):
        above.append(relay(above[-1], 1))
        below.append(relay(below[-1], -1))
    last = fetch(ratings, REACH + 1, range(0, PANELS, MEMBERS))
    near, own = pl.pallas_call(
        sums_kernel,
        out_shape=(
            jax.ShapeDtypeStruct((8, LANES), jnp.float32),
            jax.ShapeDtypeStruct((rows, width), ratings.dtype),
        ),
        in_specs=[VMEM] * 5,
        out_specs=(VMEM, VMEM),
        compiler_params=PARAMS,
        name="sums",
    )(*above[:3], *below[1:3])
    far = fetch(near, PANELS // 2)
    panels = below[:0:-1] + [own] + above[1:] + [last]

    slots = (SLOTS, SLOT_ROWS, LANES)
    lanes = jax.ShapeDtypeStruct((8, LANES), jnp.float32)
    gram = [pltpu.VMEM((6 * width, width), jnp.float32)]
    cost = pl.CostEstimate(
        flops=12 * rows * width * width, bytes_accessed=12 * rows * width, transcendentals=0
    )
    send, *known = pl.pallas_call(
        send_kernel,
        out_shape=(
            jax.ShapeDtypeStruct(slots, jnp.bfloat16),
            jax.ShapeDtypeStruct((rows, 1), jnp.float32),
            lanes,
            lanes,
        ),
        in_specs=[SMEM] + [VMEM] * 10,
        out_specs=(VMEM,) * 4,
        scratch_shapes=gram,
        compiler_params=PARAMS,
        cost_estimate=cost,
        name="send",
    )(place, near, far, *panels)
    got = lax.ppermute(send, "core", [(0, 1), (1, 0)])
    keep = pl.pallas_call(
        keep_kernel,
        out_shape=jax.ShapeDtypeStruct(slots, jnp.float32),
        in_specs=[SMEM] + [VMEM] * 11,
        out_specs=VMEM,
        scratch_shapes=gram,
        compiler_params=PARAMS,
        cost_estimate=cost,
        name="keep",
    )(place, *known, *panels)
    total = pl.pallas_call(
        add_kernel,
        out_shape=jax.ShapeDtypeStruct(slots, jnp.bfloat16),
        in_specs=[VMEM, VMEM],
        out_specs=VMEM,
        compiler_params=PARAMS,
        name="add",
    )(keep, got)
    parts = lax.all_to_all(total, "x", 0, 0, tiled=True)
    total = pl.pallas_call(
        fold_kernel,
        out_shape=jax.ShapeDtypeStruct((Y, SLOT_ROWS, LANES), jnp.bfloat16),
        in_specs=[VMEM],
        out_specs=VMEM,
        compiler_params=PARAMS,
        name="fold",
    )(parts)
    parts = lax.all_to_all(total, "y", 0, 0, tiled=True)
    block = pl.pallas_call(
        finish_kernel,
        out_shape=jax.ShapeDtypeStruct((SHARE, width), jnp.bfloat16),
        in_specs=[SMEM, VMEM],
        out_specs=VMEM,
        compiler_params=PARAMS,
        name="finish",
    )(place, parts)
    return lax.ppermute(block, AXES, homes())


def solution(mesh):
    fine = Mesh(mesh.devices.reshape(X, Y, CORES, PANELS), AXES)
    users = AXES[:3]
    return jax.shard_map(
        per_device,
        mesh=fine,
        in_specs=(P(users, "z"), P(users)),
        out_specs=P(users, "z"),
        check_vma=False,
    )
```

```python
import itertools

import jax
import jax.numpy as jnp
from jax import lax
from jax.experimental import pallas as pl
from jax.experimental.pallas import tpu as pltpu
from jax.sharding import Mesh, PartitionSpec as P

X, Y, CORES, PANELS = 4, 8, 2, 12
SLOTS = X * Y
BLOCK = 64
ITEMS = 3072
SHARE = 48
LANES = 128
SLOT_ROWS = 2 * SHARE + 8
AXES = ("x", "y", "core", "triple", "member")
COUNTS = 4
AXES = ("x", "y", "core", "z")
MEMBERS = 3
REACH = 3
UNITS = ((-3, (4, 1, 3, 2)), (-1, (2, 0, 1, -1)), (1, (-3, 0, -2, -1)))


def split_rows(total):
    high = total.astype(jnp.bfloat16).astype(jnp.float32)
    first = lax.broadcasted_iota(jnp.int32, total.shape, 0) < 4
    return jnp.where(first, high, total - high)


def join_rows(extra):
    return extra + pltpu.roll(extra, 4, 0)


def held(place_ref):
    member = lax.rem(place_ref[3], MEMBERS)
    first = sum(jnp.where(member == i, UNITS[i][0], 0) for i in range(MEMBERS))
    return member, lax.div(lax.rem(place_ref[3] + first + PANELS, PANELS), MEMBERS)


def diagonal():
    shape = (LANES, LANES)
    rows = lax.broadcasted_iota(jnp.int32, shape, 0)
    return rows == lax.broadcasted_iota(jnp.int32, shape, 1)


def own_kernel(ratings_ref, own_ref):
    own_ref[...] = ratings_ref[...]


def outer_kernel(low_ref, high_ref, out_ref):
    low, high = low_ref[...].astype(jnp.float32), high_ref[...].astype(jnp.float32)
    out_ref[...] = jnp.sum(low * low + high * high, axis=1, keepdims=True)


def sums_kernel(*refs):
    panels, sums_ref = refs[:-1], refs[-1]
    squares = jnp.zeros(panels[0].shape, jnp.float32)
    for ref in panels:
        values = ref[...].astype(jnp.float32)
        squares = squares + values * values
    upright = jnp.sum(squares, axis=1, keepdims=True)
    corner = diagonal()
    lying = [
        jnp.sum(jnp.where(corner, upright[i : i + LANES], 0.0), axis=0, keepdims=True)
        for i in range(0, upright.shape[0], LANES)
    ]
    lying.append(jnp.zeros((8 - len(lying), LANES), jnp.float32))
    sums_ref[...] = jnp.concatenate(lying, axis=0)


def weigh(scale, ref):
    values = ref[...].astype(jnp.float32)
    return values, (scale * values).astype(jnp.bfloat16)


def panel_at(panels, core, offset):
    if offset > REACH:
        return panels[-1]
    return panels[REACH - offset if core else REACH + offset]


def half_products(place_ref, scale, panels, gram_ref, partner):
    core, (member, _) = place_ref[2], held(place_ref)
    width = panels[0].shape[1]
    for its_core, its_member in itertools.product(range(CORES), range(MEMBERS)):
        first, columns = UNITS[its_member]
        at = 2 * (1 - its_core if partner else its_core)

        @pl.when((core == its_core) & (member == its_member))
        def _(its_core=its_core, first=first, columns=columns[at : at + 2]):
            for unit, offset in enumerate(columns):
                weighted = weigh(scale, panel_at(panels, its_core, offset))[1]
                for i in range(MEMBERS):
                    gram_ref[pl.ds((3 * unit + i) * width, width), :] = lax.dot_general(
                        panel_at(panels, its_core, first + i)[...],
                        weighted,
                        (((0,), (0,)), ((), ())),
                        preferred_element_type=jnp.float32,
                    )


def write_slots(place_ref, gram_ref, row_ref, column_ref, out_ref, partner):
    core, (_, triple) = place_ref[2], held(place_ref)
    width = gram_ref.shape[1]
    base = 2 * (1 - core if partner else core)
    for x in range(X):
        slot = lax.rem(triple + x, X) * Y
        for y in range(Y):
            start = (2 * y + x % 2) * SHARE
            low, high = start // LANES, (start + SHARE - 1) // LANES
            unit = x // 2
            four = [column_ref[pl.ds(2 * (base + unit) + half, 1), :] for half in range(2)]
            four += [row_ref[pl.ds(i, 1), :] for i in (low, high)]
            extra = split_rows(jnp.concatenate(four + four, axis=0))
            block = gram_ref[pl.ds(unit * 3 * width + start, SHARE), :]
            whole = jnp.concatenate([block[:, :LANES], block[:, LANES:], extra], axis=0)
            out_ref[slot + y] = whole.astype(out_ref.dtype)


def send_kernel(place_ref, near_ref, far_ref, outer_ref, *refs):
    panels, (send_ref, scale_ref, row_ref, column_ref, gram_ref) = refs[:8], refs[8:]
    core, (member, _) = place_ref[2], held(place_ref)
    rows, width = panels[0].shape
    sums = near_ref[...] + far_ref[...]
    corner = diagonal()
    square_sum = outer_ref[...] + jnp.concatenate(
        [
            jnp.sum(jnp.where(corner, sums[i : i + 1], 0.0), axis=1, keepdims=True)
            for i in range(rows // LANES)
        ],
        axis=0,
    )
    position = lax.broadcasted_iota(jnp.int32, (BLOCK, 1), 0)
    live = jnp.concatenate(
        [
            (position < place_ref[COUNTS + i]).astype(jnp.float32)
            for i in range(rows // BLOCK)
        ],
        axis=0,
    )
    scale = live / jnp.sqrt(square_sum / ITEMS + 1e-05)

    scale_ref[...] = scale

    def keep_degree(target, at, ref):
        values, weighted = weigh(scale, ref)
        total = jnp.sum(values * weighted.astype(jnp.float32), axis=0, keepdims=True)
        for half in range(2):
            lanes = total[:, half * LANES : (half + 1) * LANES]
            target[pl.ds(2 * at + half, 1), :] = lanes

    for its_core, its_member in itertools.product(range(CORES), range(MEMBERS)):
        first, columns = UNITS[its_member]

        @pl.when((core == its_core) & (member == its_member))
        def _(its_core=its_core, first=first, columns=columns):
            for i in range(MEMBERS):
                keep_degree(row_ref, i, panel_at(panels, its_core, first + i))
            for unit, offset in enumerate(columns):
                keep_degree(column_ref, unit, panel_at(panels, its_core, offset))

    half_products(place_ref, scale, panels, gram_ref, True)
    write_slots(place_ref, gram_ref, row_ref, column_ref, send_ref, True)


def keep_kernel(place_ref, scale_ref, row_ref, column_ref, *refs):
    panels, (keep_ref, gram_ref) = refs[:8], refs[8:]
    half_products(place_ref, scale_ref[...], panels, gram_ref, False)
    write_slots(place_ref, gram_ref, row_ref, column_ref, keep_ref, False)


def add_kernel(keep_ref, got_ref, out_ref):
    for slot in range(SLOTS):
        total = keep_ref[slot] + got_ref[slot].astype(jnp.float32)
        extra = split_rows(join_rows(total[2 * SHARE :]))
        out_ref[slot] = jnp.concatenate([total[: 2 * SHARE], extra], axis=0).astype(
            jnp.bfloat16
        )


def fold_kernel(got_ref, out_ref):
    for slot in range(Y):
        total = got_ref[slot].astype(jnp.float32)
        for x in range(1, X):
            total = total + got_ref[x * Y + slot].astype(jnp.float32)
        extra = split_rows(join_rows(total[2 * SHARE :]))
        out_ref[slot] = jnp.concatenate([total[: 2 * SHARE], extra], axis=0).astype(
            jnp.bfloat16
        )


def finish_kernel(place_ref, got_ref, out_ref):
    by = lax.rem(place_ref[0] - held(place_ref)[1] + X, X)
    offset = lax.rem((2 * place_ref[1] + lax.rem(by, 2)) * SHARE, LANES)
    total = got_ref[0].astype(jnp.float32)
    for slot in range(1, Y):
        total = total + got_ref[slot].astype(jnp.float32)
    extra = join_rows(total[2 * SHARE :])
    lane = lax.broadcasted_iota(jnp.int32, (SHARE, LANES), 1)
    row = lax.broadcasted_iota(jnp.int32, (SHARE, LANES), 0) + offset
    row_degree = jnp.sum(
        jnp.where(lane == row, extra[2:3], 0.0) + jnp.where(lane + LANES == row, extra[3:4], 0.0),
        axis=1,
        keepdims=True,
    )
    row_inverse = 1.0 / jnp.sqrt(row_degree)
    for half in range(2):
        block = total[half * SHARE : (half + 1) * SHARE]
        column_inverse = 1.0 / jnp.sqrt(extra[half : half + 1])
        out_ref[:, half * LANES : (half + 1) * LANES] = (
            block * row_inverse * column_inverse
        ).astype(jnp.bfloat16)


VMEM = pl.BlockSpec(memory_space=pltpu.VMEM)
SMEM = pl.BlockSpec(memory_space=pltpu.SMEM)
PARAMS = pltpu.CompilerParams(vmem_limit_bytes=48 * 1024 * 1024)


def homes():
    pairs = []
    for x in range(X):
        for y in range(Y):
            for core in range(CORES):
                for z in range(PANELS):
                    first, columns = UNITS[z % MEMBERS]
                    triple = (z + first) % PANELS // MEMBERS
                    by = (x - triple) % X
                    column = (z + columns[2 * core + by // 2]) % PANELS
                    user = 16 * triple + 2 * y + by % 2
                    source = ((x * Y + y) * CORES + core) * PANELS + z
                    pairs.append((source, user * PANELS + column))
    return pairs


def per_device(ratings, counts):
    rows, width = ratings.shape
    x, y, core, me = (lax.axis_index(name) for name in AXES)
    place = jnp.concatenate([jnp.stack([x, y, core, me]).astype(jnp.int32), counts])

    def fetch(array, by, at=range(PANELS)):
        return lax.ppermute(array, "z", [((z + by) % PANELS, z) for z in at])

    def relay(array, by):
        pairs = []
        for c in range(CORES):
            shift = -by if c else by
            pairs += [(c * PANELS + (z + shift) % PANELS, c * PANELS + z) for z in range(PANELS)]
        return lax.ppermute(array, ("core", "z"), pairs)

    own = pl.pallas_call(
        own_kernel,
        out_shape=jax.ShapeDtypeStruct((rows, width), ratings.dtype),
        in_specs=[VMEM],
        out_specs=VMEM,
        compiler_params=PARAMS,
        name="own",
    )(ratings)
    above, below = [ratings], [ratings]
    for i in range(REACH):
        above.append(relay(above[-1], 1))
        below.append(relay(below[-1], -1))
        if i == 0:
            below[1], own = lax.optimization_barrier((below[1], own))
    last = fetch(ratings, REACH + 1, range(0, PANELS, MEMBERS))
    near = pl.pallas_call(
        sums_kernel,
        out_shape=jax.ShapeDtypeStruct((8, LANES), jnp.float32),
        in_specs=[VMEM] * 5,
        out_specs=VMEM,
        compiler_params=PARAMS,
        name="sums",
    )(own, *above[1:3], *below[1:3])
    far = fetch(near, PANELS // 2)
    outer = pl.pallas_call(
        outer_kernel,
        out_shape=jax.ShapeDtypeStruct((rows, 1), jnp.float32),
        in_specs=[VMEM] * 2,
        out_specs=VMEM,
        compiler_params=PARAMS,
        name="outer",
    )(below[REACH], above[REACH])
    panels = below[:0:-1] + [own] + above[1:] + [last]

    slots = (SLOTS, SLOT_ROWS, LANES)
    lanes = jax.ShapeDtypeStruct((8, LANES), jnp.float32)
    gram = [pltpu.VMEM((6 * width, width), jnp.float32)]
    cost = pl.CostEstimate(
        flops=12 * rows * width * width, bytes_accessed=12 * rows * width, transcendentals=0
    )
    send, *known = pl.pallas_call(
        send_kernel,
        out_shape=(
            jax.ShapeDtypeStruct(slots, jnp.bfloat16),
            jax.ShapeDtypeStruct((rows, 1), jnp.float32),
            lanes,
            lanes,
        ),
        in_specs=[SMEM] + [VMEM] * 11,
        out_specs=(VMEM,) * 4,
        scratch_shapes=gram,
        compiler_params=PARAMS,
        cost_estimate=cost,
        name="send",
    )(place, near, far, outer, *panels)
    got = lax.ppermute(send, "core", [(0, 1), (1, 0)])
    keep = pl.pallas_call(
        keep_kernel,
        out_shape=jax.ShapeDtypeStruct(slots, jnp.float32),
        in_specs=[SMEM] + [VMEM] * 11,
        out_specs=VMEM,
        scratch_shapes=gram,
        compiler_params=PARAMS,
        cost_estimate=cost,
        name="keep",
    )(place, *known, *panels)
    total = pl.pallas_call(
        add_kernel,
        out_shape=jax.ShapeDtypeStruct(slots, jnp.bfloat16),
        in_specs=[VMEM, VMEM],
        out_specs=VMEM,
        compiler_params=PARAMS,
        name="add",
    )(keep, got)
    parts = lax.all_to_all(total, "x", 0, 0, tiled=True)
    total = pl.pallas_call(
        fold_kernel,
        out_shape=jax.ShapeDtypeStruct((Y, SLOT_ROWS, LANES), jnp.bfloat16),
        in_specs=[VMEM],
        out_specs=VMEM,
        compiler_params=PARAMS,
        name="fold",
    )(parts)
    parts = lax.all_to_all(total, "y", 0, 0, tiled=True)
    block = pl.pallas_call(
        finish_kernel,
        out_shape=jax.ShapeDtypeStruct((SHARE, width), jnp.bfloat16),
        in_specs=[SMEM, VMEM],
        out_specs=VMEM,
        compiler_params=PARAMS,
        name="finish",
    )(place, parts)
    return lax.ppermute(block, AXES, homes())


def solution(mesh):
    fine = Mesh(mesh.devices.reshape(X, Y, CORES, PANELS), AXES)
    users = AXES[:3]
    return jax.shard_map(
        per_device,
        mesh=fine,
        in_specs=(P(users, "z"), P(users)),
        out_specs=P(users, "z"),
        check_vma=False,
    )
```

```python
import itertools

import jax
import jax.numpy as jnp
from jax import lax
from jax.experimental import pallas as pl
from jax.experimental.pallas import tpu as pltpu
from jax.sharding import Mesh, PartitionSpec as P

X, Y, CORES, PANELS = 4, 8, 2, 12
SLOTS = X * Y
BLOCK = 64
ITEMS = 3072
SHARE = 48
LANES = 128
SLOT_ROWS = 2 * SHARE + 8
AXES = ("x", "y", "core", "triple", "member")
COUNTS = 4
AXES = ("x", "y", "core", "z")
MEMBERS = 3
REACH = 3
UNITS = ((-3, (4, 1, 3, 2)), (-1, (2, 0, 1, -1)), (1, (-3, 0, -2, -1)))


def split_rows(total):
    high = total.astype(jnp.bfloat16).astype(jnp.float32)
    first = lax.broadcasted_iota(jnp.int32, total.shape, 0) < 4
    return jnp.where(first, high, total - high)


def join_rows(extra):
    return extra + pltpu.roll(extra, 4, 0)


def held(place_ref):
    member = lax.rem(place_ref[3], MEMBERS)
    first = sum(jnp.where(member == i, UNITS[i][0], 0) for i in range(MEMBERS))
    return member, lax.div(lax.rem(place_ref[3] + first + PANELS, PANELS), MEMBERS)


def diagonal():
    shape = (LANES, LANES)
    rows = lax.broadcasted_iota(jnp.int32, shape, 0)
    return rows == lax.broadcasted_iota(jnp.int32, shape, 1)


def own_kernel(ratings_ref, own_ref):
    own_ref[...] = ratings_ref[...]


def sums_kernel(*refs):
    panels, sums_ref = refs[:-1], refs[-1]
    squares = jnp.zeros(panels[0].shape, jnp.float32)
    for ref in panels:
        values = ref[...].astype(jnp.float32)
        squares = squares + values * values
    upright = jnp.sum(squares, axis=1, keepdims=True)
    corner = diagonal()
    lying = [
        jnp.sum(jnp.where(corner, upright[i : i + LANES], 0.0), axis=0, keepdims=True)
        for i in range(0, upright.shape[0], LANES)
    ]
    lying.append(jnp.zeros((8 - len(lying), LANES), jnp.float32))
    sums_ref[...] = jnp.concatenate(lying, axis=0)


def weigh(scale, ref):
    values = ref[...].astype(jnp.float32)
    return values, (scale * values).astype(jnp.bfloat16)


def panel_at(panels, core, offset):
    if offset > REACH:
        return panels[-1]
    return panels[REACH - offset if core else REACH + offset]


def half_products(place_ref, scale, panels, gram_ref, partner):
    core, (member, _) = place_ref[2], held(place_ref)
    width = panels[0].shape[1]
    for its_core, its_member in itertools.product(range(CORES), range(MEMBERS)):
        first, columns = UNITS[its_member]
        at = 2 * (1 - its_core if partner else its_core)

        @pl.when((core == its_core) & (member == its_member))
        def _(its_core=its_core, first=first, columns=columns[at : at + 2]):
            for unit, offset in enumerate(columns):
                weighted = weigh(scale, panel_at(panels, its_core, offset))[1]
                for i in range(MEMBERS):
                    gram_ref[pl.ds((3 * unit + i) * width, width), :] = lax.dot_general(
                        panel_at(panels, its_core, first + i)[...],
                        weighted,
                        (((0,), (0,)), ((), ())),
                        preferred_element_type=jnp.float32,
                    )


def write_slots(place_ref, gram_ref, row_ref, column_ref, out_ref, partner):
    core, (_, triple) = place_ref[2], held(place_ref)
    width = gram_ref.shape[1]
    base = 2 * (1 - core if partner else core)
    for x in range(X):
        slot = lax.rem(triple + x, X) * Y
        for y in range(Y):
            start = (2 * y + x % 2) * SHARE
            low, high = start // LANES, (start + SHARE - 1) // LANES
            unit = x // 2
            four = [column_ref[pl.ds(2 * (base + unit) + half, 1), :] for half in range(2)]
            four += [row_ref[pl.ds(i, 1), :] for i in (low, high)]
            extra = split_rows(jnp.concatenate(four + four, axis=0))
            block = gram_ref[pl.ds(unit * 3 * width + start, SHARE), :]
            whole = jnp.concatenate([block[:, :LANES], block[:, LANES:], extra], axis=0)
            out_ref[slot + y] = whole.astype(out_ref.dtype)


def send_kernel(place_ref, near_ref, far_ref, *refs):
    panels, (send_ref, scale_ref, row_ref, column_ref, gram_ref) = refs[:8], refs[8:]
    core, (member, _) = place_ref[2], held(place_ref)
    rows, width = panels[0].shape
    squares = jnp.zeros((rows, width), jnp.float32)
    for ref in (panels[0], panels[2 * REACH]):
        values = ref[...].astype(jnp.float32)
        squares = squares + values * values
    sums = near_ref[...] + far_ref[...]
    corner = diagonal()
    square_sum = jnp.sum(squares, axis=1, keepdims=True) + jnp.concatenate(
        [
            jnp.sum(jnp.where(corner, sums[i : i + 1], 0.0), axis=1, keepdims=True)
            for i in range(rows // LANES)
        ],
        axis=0,
    )
    position = lax.broadcasted_iota(jnp.int32, (BLOCK, 1), 0)
    live = jnp.concatenate(
        [
            (position < place_ref[COUNTS + i]).astype(jnp.float32)
            for i in range(rows // BLOCK)
        ],
        axis=0,
    )
    scale = live / jnp.sqrt(square_sum / ITEMS + 1e-05)

    scale_ref[...] = scale

    def keep_degree(target, at, ref):
        values, weighted = weigh(scale, ref)
        total = jnp.sum(values * weighted.astype(jnp.float32), axis=0, keepdims=True)
        for half in range(2):
            lanes = total[:, half * LANES : (half + 1) * LANES]
            target[pl.ds(2 * at + half, 1), :] = lanes

    for its_core, its_member in itertools.product(range(CORES), range(MEMBERS)):
        first, columns = UNITS[its_member]

        @pl.when((core == its_core) & (member == its_member))
        def _(its_core=its_core, first=first, columns=columns):
            for i in range(MEMBERS):
                keep_degree(row_ref, i, panel_at(panels, its_core, first + i))
            for unit, offset in enumerate(columns):
                keep_degree(column_ref, unit, panel_at(panels, its_core, offset))

    half_products(place_ref, scale, panels, gram_ref, True)
    write_slots(place_ref, gram_ref, row_ref, column_ref, send_ref, True)


def keep_kernel(place_ref, scale_ref, row_ref, column_ref, *refs):
    panels, (keep_ref, gram_ref) = refs[:8], refs[8:]
    half_products(place_ref, scale_ref[...], panels, gram_ref, False)
    write_slots(place_ref, gram_ref, row_ref, column_ref, keep_ref, False)


def add_kernel(keep_ref, got_ref, out_ref):
    for slot in range(SLOTS):
        total = keep_ref[slot] + got_ref[slot].astype(jnp.float32)
        extra = split_rows(join_rows(total[2 * SHARE :]))
        out_ref[slot] = jnp.concatenate([total[: 2 * SHARE], extra], axis=0).astype(
            jnp.bfloat16
        )


def fold_kernel(got_ref, out_ref):
    for slot in range(Y):
        total = got_ref[slot].astype(jnp.float32)
        for x in range(1, X):
            total = total + got_ref[x * Y + slot].astype(jnp.float32)
        extra = split_rows(join_rows(total[2 * SHARE :]))
        out_ref[slot] = jnp.concatenate([total[: 2 * SHARE], extra], axis=0).astype(
            jnp.bfloat16
        )


def finish_kernel(place_ref, got_ref, out_ref):
    by = lax.rem(place_ref[0] - held(place_ref)[1] + X, X)
    offset = lax.rem((2 * place_ref[1] + lax.rem(by, 2)) * SHARE, LANES)
    total = got_ref[0].astype(jnp.float32)
    for slot in range(1, Y):
        total = total + got_ref[slot].astype(jnp.float32)
    extra = join_rows(total[2 * SHARE :])
    lane = lax.broadcasted_iota(jnp.int32, (SHARE, LANES), 1)
    row = lax.broadcasted_iota(jnp.int32, (SHARE, LANES), 0) + offset
    row_degree = jnp.sum(
        jnp.where(lane == row, extra[2:3], 0.0) + jnp.where(lane + LANES == row, extra[3:4], 0.0),
        axis=1,
        keepdims=True,
    )
    row_inverse = 1.0 / jnp.sqrt(row_degree)
    for half in range(2):
        block = total[half * SHARE : (half + 1) * SHARE]
        column_inverse = 1.0 / jnp.sqrt(extra[half : half + 1])
        out_ref[:, half * LANES : (half + 1) * LANES] = (
            block * row_inverse * column_inverse
        ).astype(jnp.bfloat16)


VMEM = pl.BlockSpec(memory_space=pltpu.VMEM)
SMEM = pl.BlockSpec(memory_space=pltpu.SMEM)
PARAMS = pltpu.CompilerParams(vmem_limit_bytes=48 * 1024 * 1024)


def homes():
    pairs = []
    for x in range(X):
        for y in range(Y):
            for core in range(CORES):
                for z in range(PANELS):
                    first, columns = UNITS[z % MEMBERS]
                    triple = (z + first) % PANELS // MEMBERS
                    by = (x - triple) % X
                    column = (z + columns[2 * core + by // 2]) % PANELS
                    user = 16 * triple + 2 * y + by % 2
                    source = ((x * Y + y) * CORES + core) * PANELS + z
                    pairs.append((source, user * PANELS + column))
    return pairs


def per_device(ratings, counts):
    rows, width = ratings.shape
    x, y, core, me = (lax.axis_index(name) for name in AXES)
    place = jnp.concatenate([jnp.stack([x, y, core, me]).astype(jnp.int32), counts])

    def fetch(array, by, at=range(PANELS)):
        return lax.ppermute(array, "z", [((z + by) % PANELS, z) for z in at])

    def relay(array, by):
        pairs = []
        for c in range(CORES):
            shift = -by if c else by
            pairs += [(c * PANELS + (z + shift) % PANELS, c * PANELS + z) for z in range(PANELS)]
        return lax.ppermute(array, ("core", "z"), pairs)

    own = pl.pallas_call(
        own_kernel,
        out_shape=jax.ShapeDtypeStruct((rows, width), ratings.dtype),
        in_specs=[VMEM],
        out_specs=VMEM,
        compiler_params=PARAMS,
        name="own",
    )(ratings)
    above, below = [ratings], [ratings]
    for i in range(REACH):
        above.append(relay(above[-1], 1))
        below.append(relay(below[-1], -1))
        if i == 0:
            below[1], own = lax.optimization_barrier((below[1], own))
    last = fetch(ratings, REACH + 1, range(0, PANELS, MEMBERS))
    near = pl.pallas_call(
        sums_kernel,
        out_shape=jax.ShapeDtypeStruct((8, LANES), jnp.float32),
        in_specs=[VMEM] * 5,
        out_specs=VMEM,
        compiler_params=PARAMS,
        name="sums",
    )(own, *above[1:3], *below[1:3])
    far = fetch(near, PANELS // 2)
    panels = below[:0:-1] + [own] + above[1:] + [last]

    slots = (SLOTS, SLOT_ROWS, LANES)
    lanes = jax.ShapeDtypeStruct((8, LANES), jnp.float32)
    gram = [pltpu.VMEM((6 * width, width), jnp.float32)]
    cost = pl.CostEstimate(
        flops=12 * rows * width * width, bytes_accessed=12 * rows * width, transcendentals=0
    )
    send, *known = pl.pallas_call(
        send_kernel,
        out_shape=(
            jax.ShapeDtypeStruct(slots, jnp.bfloat16),
            jax.ShapeDtypeStruct((rows, 1), jnp.float32),
            lanes,
            lanes,
        ),
        in_specs=[SMEM] + [VMEM] * 10,
        out_specs=(VMEM,) * 4,
        scratch_shapes=gram,
        compiler_params=PARAMS,
        cost_estimate=cost,
        name="send",
    )(place, near, far, *panels)
    got = lax.ppermute(send, "core", [(0, 1), (1, 0)])
    keep = pl.pallas_call(
        keep_kernel,
        out_shape=jax.ShapeDtypeStruct(slots, jnp.float32),
        in_specs=[SMEM] + [VMEM] * 11,
        out_specs=VMEM,
        scratch_shapes=gram,
        compiler_params=PARAMS,
        cost_estimate=cost,
        name="keep",
    )(place, *known, *panels)
    total = pl.pallas_call(
        add_kernel,
        out_shape=jax.ShapeDtypeStruct(slots, jnp.bfloat16),
        in_specs=[VMEM, VMEM],
        out_specs=VMEM,
        compiler_params=PARAMS,
        name="add",
    )(keep, got)
    parts = lax.all_to_all(total, "x", 0, 0, tiled=True)
    total = pl.pallas_call(
        fold_kernel,
        out_shape=jax.ShapeDtypeStruct((Y, SLOT_ROWS, LANES), jnp.bfloat16),
        in_specs=[VMEM],
        out_specs=VMEM,
        compiler_params=PARAMS,
        name="fold",
    )(parts)
    parts = lax.all_to_all(total, "y", 0, 0, tiled=True)
    block = pl.pallas_call(
        finish_kernel,
        out_shape=jax.ShapeDtypeStruct((SHARE, width), jnp.bfloat16),
        in_specs=[SMEM, VMEM],
        out_specs=VMEM,
        compiler_params=PARAMS,
        name="finish",
    )(place, parts)
    return lax.ppermute(block, AXES, homes())


def solution(mesh):
    fine = Mesh(mesh.devices.reshape(X, Y, CORES, PANELS), AXES)
    users = AXES[:3]
    return jax.shard_map(
        per_device,
        mesh=fine,
        in_specs=(P(users, "z"), P(users)),
        out_specs=P(users, "z"),
        check_vma=False,
    )
```

```python
import itertools

import jax
import jax.numpy as jnp
from jax import lax
from jax.experimental import pallas as pl
from jax.experimental.pallas import tpu as pltpu
from jax.sharding import Mesh, PartitionSpec as P

X, Y, CORES, PANELS = 4, 8, 2, 12
SLOTS = X * Y
BLOCK = 64
ITEMS = 3072
SHARE = 48
LANES = 128
SLOT_ROWS = 2 * SHARE + 8
AXES = ("x", "y", "core", "triple", "member")
COUNTS = 4
AXES = ("x", "y", "core", "z")
MEMBERS = 3
REACH = 3
UNITS = ((-3, (4, 1, 3, 2)), (-1, (2, 0, 1, -1)), (1, (-3, 0, -2, -1)))


def split_rows(total):
    high = total.astype(jnp.bfloat16).astype(jnp.float32)
    first = lax.broadcasted_iota(jnp.int32, total.shape, 0) < 4
    return jnp.where(first, high, total - high)


def join_rows(extra):
    return extra + pltpu.roll(extra, 4, 0)


def held(place_ref):
    member = lax.rem(place_ref[3], MEMBERS)
    first = sum(jnp.where(member == i, UNITS[i][0], 0) for i in range(MEMBERS))
    return member, lax.div(lax.rem(place_ref[3] + first + PANELS, PANELS), MEMBERS)


def diagonal():
    shape = (LANES, LANES)
    rows = lax.broadcasted_iota(jnp.int32, shape, 0)
    return rows == lax.broadcasted_iota(jnp.int32, shape, 1)


def own_kernel(ratings_ref, own_ref):
    own_ref[...] = ratings_ref[...]


def sums_kernel(*refs):
    panels, sums_ref = refs[:-1], refs[-1]
    squares = jnp.zeros(panels[0].shape, jnp.float32)
    for ref in panels:
        values = ref[...].astype(jnp.float32)
        squares = squares + values * values
    upright = jnp.sum(squares, axis=1, keepdims=True)
    corner = diagonal()
    lying = [
        jnp.sum(jnp.where(corner, upright[i : i + LANES], 0.0), axis=0, keepdims=True)
        for i in range(0, upright.shape[0], LANES)
    ]
    lying.append(jnp.zeros((8 - len(lying), LANES), jnp.float32))
    sums_ref[...] = jnp.concatenate(lying, axis=0)


def weigh(scale, ref):
    values = ref[...].astype(jnp.float32)
    return values, (scale * values).astype(jnp.bfloat16)


def panel_at(panels, core, offset):
    if offset > REACH:
        return panels[-1]
    return panels[REACH + offset if core else REACH - offset]


def half_products(place_ref, scale, panels, gram_ref, partner):
    core, (member, _) = place_ref[2], held(place_ref)
    width = panels[0].shape[1]
    for its_core, its_member in itertools.product(range(CORES), range(MEMBERS)):
        first, columns = UNITS[its_member]
        at = 2 * (1 - its_core if partner else its_core)

        @pl.when((core == its_core) & (member == its_member))
        def _(its_core=its_core, first=first, columns=columns[at : at + 2]):
            for unit, offset in enumerate(columns):
                weighted = weigh(scale, panel_at(panels, its_core, offset))[1]
                for i in range(MEMBERS):
                    gram_ref[pl.ds((3 * unit + i) * width, width), :] = lax.dot_general(
                        panel_at(panels, its_core, first + i)[...],
                        weighted,
                        (((0,), (0,)), ((), ())),
                        preferred_element_type=jnp.float32,
                    )


def write_slots(place_ref, gram_ref, row_ref, column_ref, out_ref, partner):
    core, (_, triple) = place_ref[2], held(place_ref)
    width = gram_ref.shape[1]
    base = 2 * (1 - core if partner else core)
    for x in range(X):
        slot = lax.rem(triple + x, X) * Y
        for y in range(Y):
            start = (2 * y + x % 2) * SHARE
            low, high = start // LANES, (start + SHARE - 1) // LANES
            unit = x // 2
            four = [column_ref[pl.ds(2 * (base + unit) + half, 1), :] for half in range(2)]
            four += [row_ref[pl.ds(i, 1), :] for i in (low, high)]
            extra = split_rows(jnp.concatenate(four + four, axis=0))
            block = gram_ref[pl.ds(unit * 3 * width + start, SHARE), :]
            whole = jnp.concatenate([block[:, :LANES], block[:, LANES:], extra], axis=0)
            out_ref[slot + y] = whole.astype(out_ref.dtype)


def send_kernel(place_ref, near_ref, far_ref, *refs):
    panels, (send_ref, scale_ref, row_ref, column_ref, gram_ref) = refs[:8], refs[8:]
    core, (member, _) = place_ref[2], held(place_ref)
    rows, width = panels[0].shape
    squares = jnp.zeros((rows, width), jnp.float32)
    for ref in (panels[0], panels[2 * REACH]):
        values = ref[...].astype(jnp.float32)
        squares = squares + values * values
    sums = near_ref[...] + far_ref[...]
    corner = diagonal()
    square_sum = jnp.sum(squares, axis=1, keepdims=True) + jnp.concatenate(
        [
            jnp.sum(jnp.where(corner, sums[i : i + 1], 0.0), axis=1, keepdims=True)
            for i in range(rows // LANES)
        ],
        axis=0,
    )
    position = lax.broadcasted_iota(jnp.int32, (BLOCK, 1), 0)
    live = jnp.concatenate(
        [
            (position < place_ref[COUNTS + i]).astype(jnp.float32)
            for i in range(rows // BLOCK)
        ],
        axis=0,
    )
    scale = live / jnp.sqrt(square_sum / ITEMS + 1e-05)

    scale_ref[...] = scale

    def keep_degree(target, at, ref):
        values, weighted = weigh(scale, ref)
        total = jnp.sum(values * weighted.astype(jnp.float32), axis=0, keepdims=True)
        for half in range(2):
            lanes = total[:, half * LANES : (half + 1) * LANES]
            target[pl.ds(2 * at + half, 1), :] = lanes

    for its_core, its_member in itertools.product(range(CORES), range(MEMBERS)):
        first, columns = UNITS[its_member]

        @pl.when((core == its_core) & (member == its_member))
        def _(its_core=its_core, first=first, columns=columns):
            for i in range(MEMBERS):
                keep_degree(row_ref, i, panel_at(panels, its_core, first + i))
            for unit, offset in enumerate(columns):
                keep_degree(column_ref, unit, panel_at(panels, its_core, offset))

    half_products(place_ref, scale, panels, gram_ref, True)
    write_slots(place_ref, gram_ref, row_ref, column_ref, send_ref, True)


def keep_kernel(place_ref, scale_ref, row_ref, column_ref, *refs):
    panels, (keep_ref, gram_ref) = refs[:8], refs[8:]
    half_products(place_ref, scale_ref[...], panels, gram_ref, False)
    write_slots(place_ref, gram_ref, row_ref, column_ref, keep_ref, False)


def add_kernel(keep_ref, got_ref, out_ref):
    for slot in range(SLOTS):
        total = keep_ref[slot] + got_ref[slot].astype(jnp.float32)
        extra = split_rows(join_rows(total[2 * SHARE :]))
        out_ref[slot] = jnp.concatenate([total[: 2 * SHARE], extra], axis=0).astype(
            jnp.bfloat16
        )


def fold_kernel(got_ref, out_ref):
    for slot in range(Y):
        total = got_ref[slot].astype(jnp.float32)
        for x in range(1, X):
            total = total + got_ref[x * Y + slot].astype(jnp.float32)
        extra = split_rows(join_rows(total[2 * SHARE :]))
        out_ref[slot] = jnp.concatenate([total[: 2 * SHARE], extra], axis=0).astype(
            jnp.bfloat16
        )


def finish_kernel(place_ref, got_ref, out_ref):
    by = lax.rem(place_ref[0] - held(place_ref)[1] + X, X)
    offset = lax.rem((2 * place_ref[1] + lax.rem(by, 2)) * SHARE, LANES)
    total = got_ref[0].astype(jnp.float32)
    for slot in range(1, Y):
        total = total + got_ref[slot].astype(jnp.float32)
    extra = join_rows(total[2 * SHARE :])
    lane = lax.broadcasted_iota(jnp.int32, (SHARE, LANES), 1)
    row = lax.broadcasted_iota(jnp.int32, (SHARE, LANES), 0) + offset
    row_degree = jnp.sum(
        jnp.where(lane == row, extra[2:3], 0.0) + jnp.where(lane + LANES == row, extra[3:4], 0.0),
        axis=1,
        keepdims=True,
    )
    row_inverse = 1.0 / jnp.sqrt(row_degree)
    for half in range(2):
        block = total[half * SHARE : (half + 1) * SHARE]
        column_inverse = 1.0 / jnp.sqrt(extra[half : half + 1])
        out_ref[:, half * LANES : (half + 1) * LANES] = (
            block * row_inverse * column_inverse
        ).astype(jnp.bfloat16)


VMEM = pl.BlockSpec(memory_space=pltpu.VMEM)
SMEM = pl.BlockSpec(memory_space=pltpu.SMEM)
PARAMS = pltpu.CompilerParams(vmem_limit_bytes=48 * 1024 * 1024)


def homes():
    pairs = []
    for x in range(X):
        for y in range(Y):
            for core in range(CORES):
                for z in range(PANELS):
                    first, columns = UNITS[z % MEMBERS]
                    triple = (z + first) % PANELS // MEMBERS
                    by = (x - triple) % X
                    column = (z + columns[2 * core + by // 2]) % PANELS
                    user = 16 * triple + 2 * y + by % 2
                    source = ((x * Y + y) * CORES + core) * PANELS + z
                    pairs.append((source, user * PANELS + column))
    return pairs


def per_device(ratings, counts):
    rows, width = ratings.shape
    x, y, core, me = (lax.axis_index(name) for name in AXES)
    place = jnp.concatenate([jnp.stack([x, y, core, me]).astype(jnp.int32), counts])

    def fetch(array, by, at=range(PANELS)):
        return lax.ppermute(array, "z", [((z + by) % PANELS, z) for z in at])

    def relay(array, by):
        pairs = []
        for c in range(CORES):
            shift = by if c else -by
            pairs += [(c * PANELS + (z + shift) % PANELS, c * PANELS + z) for z in range(PANELS)]
        return lax.ppermute(array, ("core", "z"), pairs)

    own = pl.pallas_call(
        own_kernel,
        out_shape=jax.ShapeDtypeStruct((rows, width), ratings.dtype),
        in_specs=[VMEM],
        out_specs=VMEM,
        compiler_params=PARAMS,
        name="own",
    )(ratings)
    above, below = [ratings], [ratings]
    for i in range(REACH):
        above.append(relay(above[-1], 1))
        below.append(relay(below[-1], -1))
        if i == 0:
            below[1], own = lax.optimization_barrier((below[1], own))
    last = fetch(ratings, REACH + 1, range(0, PANELS, MEMBERS))
    near = pl.pallas_call(
        sums_kernel,
        out_shape=jax.ShapeDtypeStruct((8, LANES), jnp.float32),
        in_specs=[VMEM] * 5,
        out_specs=VMEM,
        compiler_params=PARAMS,
        name="sums",
    )(own, *above[1:3], *below[1:3])
    far = fetch(near, PANELS // 2)
    panels = below[:0:-1] + [own] + above[1:] + [last]

    slots = (SLOTS, SLOT_ROWS, LANES)
    lanes = jax.ShapeDtypeStruct((8, LANES), jnp.float32)
    gram = [pltpu.VMEM((6 * width, width), jnp.float32)]
    cost = pl.CostEstimate(
        flops=12 * rows * width * width, bytes_accessed=12 * rows * width, transcendentals=0
    )
    send, *known = pl.pallas_call(
        send_kernel,
        out_shape=(
            jax.ShapeDtypeStruct(slots, jnp.bfloat16),
            jax.ShapeDtypeStruct((rows, 1), jnp.float32),
            lanes,
            lanes,
        ),
        in_specs=[SMEM] + [VMEM] * 10,
        out_specs=(VMEM,) * 4,
        scratch_shapes=gram,
        compiler_params=PARAMS,
        cost_estimate=cost,
        name="send",
    )(place, near, far, *panels)
    got = lax.ppermute(send, "core", [(0, 1), (1, 0)])
    keep = pl.pallas_call(
        keep_kernel,
        out_shape=jax.ShapeDtypeStruct(slots, jnp.float32),
        in_specs=[SMEM] + [VMEM] * 11,
        out_specs=VMEM,
        scratch_shapes=gram,
        compiler_params=PARAMS,
        cost_estimate=cost,
        name="keep",
    )(place, *known, *panels)
    total = pl.pallas_call(
        add_kernel,
        out_shape=jax.ShapeDtypeStruct(slots, jnp.bfloat16),
        in_specs=[VMEM, VMEM],
        out_specs=VMEM,
        compiler_params=PARAMS,
        name="add",
    )(keep, got)
    parts = lax.all_to_all(total, "x", 0, 0, tiled=True)
    total = pl.pallas_call(
        fold_kernel,
        out_shape=jax.ShapeDtypeStruct((Y, SLOT_ROWS, LANES), jnp.bfloat16),
        in_specs=[VMEM],
        out_specs=VMEM,
        compiler_params=PARAMS,
        name="fold",
    )(parts)
    parts = lax.all_to_all(total, "y", 0, 0, tiled=True)
    block = pl.pallas_call(
        finish_kernel,
        out_shape=jax.ShapeDtypeStruct((SHARE, width), jnp.bfloat16),
        in_specs=[SMEM, VMEM],
        out_specs=VMEM,
        compiler_params=PARAMS,
        name="finish",
    )(place, parts)
    return lax.ppermute(block, AXES, homes())


def solution(mesh):
    fine = Mesh(mesh.devices.reshape(X, Y, CORES, PANELS), AXES)
    users = AXES[:3]
    return jax.shard_map(
        per_device,
        mesh=fine,
        in_specs=(P(users, "z"), P(users)),
        out_specs=P(users, "z"),
        check_vma=False,
    )
```
